32 devices in a mesh: shard: 4 (over y, x), ctx: 2 (over core), tp: 4 (over z).
Axes of the slice: x: 2, y: 2, z: 4, core: 2. Of those that a mesh axis runs over, the one named last changes fastest.
Arguments:
- latent: bfloat16 [4, 4096, 768], P('shard', ('ctx', 'tp')), may hold values from -6 to 6
- condition: bfloat16 [4, 768], P('shard'), may hold values from -6 to 6
- modulator: bfloat16 [768, 4608], P('shard'), may hold values from -0.21875 to 0.21875
- modulator_bias: bfloat16 [4608], replicated, may hold values from -3 to 3
- projector: bfloat16 [768, 3, 768], P('shard', None, 'tp'), may hold values from -0.21875 to 0.21875
- projector_bias: bfloat16 [2, 768], P(None, 'tp'), may hold values from -3 to 3
- merger: bfloat16 [768, 768], P('tp', 'shard'), may hold values from -3 to 3
- merger_bias: bfloat16 [768], replicated, may hold values from -3 to 3
- expander: bfloat16 [768, 3072], P('shard', 'tp'), may hold values from -0.21875 to 0.21875
- expander_bias: bfloat16 [3072], P('tp'), may hold values from -3 to 3
- reducer: bfloat16 [3072, 768], P('tp', 'shard'), may hold values from -0.109375 to 0.109375
- reducer_bias: bfloat16 [768], replicated, may hold values from -3 to 3
- cotangent: bfloat16 [4, 4096, 768], P('shard', ('ctx', 'tp')), may hold values from -6 to 6
Outputs:
- block_output: bfloat16 [4, 4096, 768], P('shard', ('ctx', 'tp'))
- grad_latent: float32 [4, 4096, 768], P('shard', ('ctx', 'tp'))
- grad_condition: float32 [4, 768], P('shard')
- grad_modulator: float32 [768, 4608], P(('shard', 'ctx'), 'tp')
- grad_modulator_bias: float32 [4608], P('tp')
- grad_projector: float32 [768, 3, 768], P(('shard', 'ctx'), None, 'tp')
- grad_projector_bias: float32 [2, 768], P(None, 'tp')
- grad_merger: float32 [768, 768], P('tp', ('shard', 'ctx'))
- grad_merger_bias: float32 [768], replicated
- grad_expander: float32 [768, 3072], P(('shard', 'ctx'), 'tp')
- grad_expander_bias: float32 [3072], P('tp')
- grad_reducer: float32 [3072, 768], P('tp', ('shard', 'ctx'))
- grad_reducer_bias: float32 [768], replicated
The draws below stay inside these ranges and needn't reach their ends.
All inputs are finite; a program needn't handle non-finite values.
Results may differ from the reference program's by a relative error of at most 0.015.
The reference program's roundings to bfloat16 on the way count: a program that leaves them out, or rounds other values in their place, can miss the bound.
Values may be sent and summed in bfloat16 or wider, within the bound.
No kernel may reach another device: no remote copies, remote signals or barrier semaphores. Data moves between devices by JAX's collectives and lax.ppermute only.
A program may use at most 256 MiB of HBM per device.

```python
import math
import jax
import jax.numpy as jnp
from jax import lax

D = 768
HEAD_DIM = 64
FF = 3072
L = 4096
IMAGES = 4


def block_levels(own_key, dims, cuts, smallest, top_value):
    loudness, own = 1.0, jax.random.fold_in(own_key, 6)
    for dim, parts in cuts:
        draws = jnp.exp(jax.random.uniform(jax.random.fold_in(own, dim), (parts,), jnp.float32, smallest / len(cuts), top_value / len(cuts)))
        loudness = loudness * jnp.repeat(draws, dims[dim] // parts).reshape([-1 if axis == dim else 1 for axis in range(len(dims))])
    return loudness


def bell_draw(stream_key, dims, spread, reach, pieces=(), held_as=jnp.bfloat16):
    drawn = jax.random.normal(stream_key, dims, jnp.float32) * spread
    if len(pieces) > 0:
        drawn = block_levels(stream_key, dims, pieces, -0.22, 0.18) * drawn
    return jnp.clip(drawn, min=-reach, max=reach).astype(held_as)


def setup_inputs(seed: int = 0) -> dict:
    seeds = jax.random.split(jax.random.key(seed), 14)
    latent = bell_draw(seeds[0], (IMAGES, L, D), 1.0, 6.0, ((0, 4), (1, 8)))
    condition = bell_draw(seeds[1], (IMAGES, D), 1.0, 6.0, ((0, 4),))
    modulator = bell_draw(seeds[2], (D, 6 * D), D ** -0.5, 0.21875, ((0, 4),))
    modulator_bias = bell_draw(seeds[3], (6 * D,), 0.5, 3.0)
    projector = bell_draw(seeds[4], (D, 3, D), D ** -0.5, 0.21875, ((0, 4), (2, 4)))
    projector_bias = bell_draw(seeds[5], (2, D), 0.5, 3.0, ((1, 4),))
    merger = bell_draw(seeds[6], (D, D), (max(D // 192, 1)) ** -0.5, 3.0, ((0, 4), (1, 4)))
    merger_bias = bell_draw(seeds[7], (D,), 0.5, 3.0)
    expander = bell_draw(seeds[8], (D, FF), D ** -0.5, 0.21875, ((0, 4), (1, 4)))
    expander_bias = bell_draw(seeds[9], (FF,), 0.5, 3.0, ((0, 4),))
    reducer = bell_draw(seeds[10], (FF, D), FF ** -0.5, 0.109375, ((0, 4), (1, 4)))
    reducer_bias = bell_draw(seeds[11], (D,), 0.5, 3.0)
    cotangent = bell_draw(seeds[12], (IMAGES, L, D), 1.0, 6.0, ((0, 4), (1, 8)))
    return dict(latent=latent, condition=condition, modulator=modulator, modulator_bias=modulator_bias, projector=projector, projector_bias=projector_bias, merger=merger, merger_bias=merger_bias, expander=expander, expander_bias=expander_bias, reducer=reducer, reducer_bias=reducer_bias, cotangent=cotangent)


PRECISE = lax.Precision.HIGHEST

@jax.custom_vjp
def low(v):
    return lax.optimization_barrier(v.astype(jnp.bfloat16)).astype(jnp.float32)

@jax.custom_vjp
def low_back(v):
    return v

def low_keep(v):
    return (low(v), None)

def low_pass(kept, grad):
    return (grad,)

def back_keep(v):
    return (v, None)

def back_low(kept, grad):
    return (low(grad),)
low.defvjp(low_keep, low_pass)
low_back.defvjp(back_keep, back_low)

def layer_norm(values):
    row_mean = lax.optimization_barrier(jnp.mean(values, -1, keepdims=True))
    centered = values - row_mean
    variance = lax.optimization_barrier(jnp.mean(centered * centered, -1, keepdims=True))
    return centered * lax.rsqrt(variance + 1e-06)

def gelu_tanh(values):
    return 0.5 * values * (1.0 + jnp.tanh(0.7978845608028654 * (values + 0.044715 * values * values * values)))

def silu_gate(values):
    return values * jax.nn.sigmoid(values)

def attend_head(operands):
    query_head, key_head, value_head = operands
    scores = low_back(jnp.dot(query_head, key_head.T, precision=PRECISE) * HEAD_DIM ** (-0.5))
    exponent = jnp.exp(scores - lax.optimization_barrier(jnp.max(scores, -1, keepdims=True)))
    softmaxed = exponent / lax.optimization_barrier(jnp.sum(exponent, -1, keepdims=True))
    return jnp.dot(low(softmaxed), value_head, precision=PRECISE)

def attend_image(operands):
    queries, key_rows, value_rows = operands
    token_count, model_width = queries.shape
    head_count = model_width // HEAD_DIM

    def by_head(array):
        return array.reshape(-1, head_count, HEAD_DIM).transpose(1, 0, 2)
    mixed = lax.map(jax.checkpoint(attend_head), (by_head(queries), by_head(key_rows), by_head(value_rows)))
    return mixed.transpose(1, 0, 2).reshape(token_count, model_width)

def group_forward(latent, settings, projector, projector_bias, merger, merger_bias, expander, expander_bias, reducer, reducer_bias):
    model_width = latent.shape[-1]
    shift_one = settings[:, None, 0:model_width]
    scale_one = settings[:, None, model_width:2 * model_width]
    gate_one = settings[:, None, 2 * model_width:3 * model_width]
    shift_two = settings[:, None, 3 * model_width:4 * model_width]
    scale_two = settings[:, None, 4 * model_width:5 * model_width]
    gate_two = settings[:, None, 5 * model_width:6 * model_width]
    normed = low(layer_norm(latent) * (1.0 + scale_one) + shift_one)
    queries = low(low_back(jnp.einsum('btd,de->bte', normed, projector[:, 0, :], precision=PRECISE) + projector_bias[0]))
    key_rows = low(low_back(jnp.einsum('btd,de->bte', normed, projector[:, 1, :], precision=PRECISE)))
    value_rows = low(low_back(jnp.einsum('btd,de->bte', normed, projector[:, 2, :], precision=PRECISE) + projector_bias[1]))
    attended = lax.map(attend_image, (queries, key_rows, value_rows))
    attended = low(low_back(attended))
    branch = low_back(jnp.einsum('btd,de->bte', attended, merger, precision=PRECISE) + merger_bias)
    middle = latent + gate_one * branch
    normed_two = low(layer_norm(middle) * (1.0 + scale_two) + shift_two)
    hidden = low_back(jnp.einsum('btd,df->btf', normed_two, expander, precision=PRECISE) + expander_bias)
    activated = low(gelu_tanh(hidden))
    feed = low_back(jnp.einsum('btf,fd->btd', activated, reducer, precision=PRECISE) + reducer_bias)
    return middle + gate_two * feed

def forward(latent, condition, modulator, modulator_bias, projector, projector_bias, merger, merger_bias, expander, expander_bias, reducer, reducer_bias):
    scaled = low(silu_gate(condition))
    modulation = jnp.dot(scaled, modulator, precision=PRECISE) + modulator_bias
    images, length, model_width = latent.shape
    group_size = math.gcd(images, max(1, 4096 // length))
    grouped = latent.reshape(images // group_size, group_size, length, model_width)
    settings = modulation.reshape(images // group_size, group_size, modulation.shape[1])

    def run_group(operands):
        return group_forward(operands[0], operands[1], projector, projector_bias, merger, merger_bias, expander, expander_bias, reducer, reducer_bias)
    results = lax.map(jax.checkpoint(run_group), (grouped, settings))
    return results.reshape(latent.shape)

def reference(latent, condition, modulator, modulator_bias, projector, projector_bias, merger, merger_bias, expander, expander_bias, reducer, reducer_bias, cotangent):
    inputs = tuple((array.astype(jnp.float32) for array in (latent, condition, modulator, modulator_bias, projector, projector_bias, merger, merger_bias, expander, expander_bias, reducer, reducer_bias)))
    result, pullback = jax.vjp(forward, *inputs)
    gradients = pullback(cotangent.astype(jnp.float32))
    return (result.astype(jnp.bfloat16), gradients[0], gradients[1], gradients[2], gradients[3], gradients[4], gradients[5], gradients[6], gradients[7], gradients[8], gradients[9], gradients[10], gradients[11])
```

```python
import functools
import math

import jax
import jax.numpy as jnp
from jax import lax
from jax.experimental import pallas as pl
from jax.experimental.pallas import tpu as pltpu
from jax.sharding import PartitionSpec as P

HEAD_DIM = 64
PRECISE = lax.Precision.HIGHEST
LOW = jnp.bfloat16
WIDE = jnp.float32


def layer_norm(values):
    row_mean = jnp.mean(values, -1, keepdims=True)
    centered = values - row_mean
    variance = jnp.mean(centered * centered, -1, keepdims=True)
    return centered * lax.rsqrt(variance + 1e-06)


def gelu_tanh(values):
    return (
        0.5
        * values
        * (1.0 + jnp.tanh(0.7978845608028654 * (values + 0.044715 * values * values * values)))
    )


def silu_gate(values):
    return values * jax.nn.sigmoid(values)


def modulate(values, scale_part, shift_part):
    return layer_norm(values) * (1.0 + scale_part) + shift_part


def dot_wide(left, right, left_dim, right_dim):
    return lax.dot_general(
        left, right, (((left_dim,), (right_dim,)), ((), ())), preferred_element_type=WIDE
    )


def gather_list(block, axis):
    count = lax.axis_size(axis)
    return [block] + [
        lax.ppermute(block, axis, [(i, (i - r) % count) for i in range(count)])
        for r in range(1, count)
    ]


def scatter_list(blocks, axis):
    count = lax.axis_size(axis)
    arrived = {
        (count - r) % count: lax.ppermute(
            blocks[r], axis, [(i, (i + r) % count) for i in range(count)]
        )
        for r in range(1, count)
    }
    arrived[0] = blocks[0]
    return [arrived[r] for r in range(count)]


def swap_ctx(block):
    count = lax.axis_size("ctx")
    return lax.ppermute(block, "ctx", [(i, (i + 1) % count) for i in range(count)])


def sum_over(value, axes):
    for axis in axes:
        step = 1
        while step < lax.axis_size(axis):
            value = value + lax.ppermute(
                value, axis, [(i, i ^ step) for i in range(lax.axis_size(axis))]
            )
            step *= 2
    return value


def after(value, *earlier):
    return lax.optimization_barrier((value,) + tuple(earlier))[0]


def attend_kernel(query_ref, key_ref, value_ref, far_key_ref, far_value_ref, out_ref, stat_ref, key_rows):
    near = key_ref.shape[2]
    key_rows[:near, :] = key_ref[0].T
    key_rows[near:, :] = far_key_ref[0].T
    queries = query_ref[0] * jnp.array(HEAD_DIM ** (-0.5), LOW)
    columns = queries.shape[1]
    top = total = mixed = None
    for half, values in enumerate((value_ref, far_value_ref)):
        scores = jnp.dot(
            key_rows[half * near : (half + 1) * near, :], queries, preferred_element_type=WIDE
        )
        block_top = jnp.max(scores, 0, keepdims=True)
        new_top = block_top if top is None else jnp.maximum(top, block_top)
        exponent = jnp.exp(scores - new_top)
        block_total = jnp.sum(exponent, 0, keepdims=True)
        block_mixed = jnp.dot(values[0], exponent.astype(LOW), preferred_element_type=WIDE)
        if top is None:
            total, mixed = block_total, block_mixed
        else:
            fade = jnp.exp(top - new_top)
            total = total * fade + block_total
            mixed = mixed * fade + block_mixed
        top = new_top
    out_ref[0] = (mixed / total).astype(LOW)
    stat_ref[0] = top + jnp.log(total)


def attend(near_rows, far_rows, place, width):
    heads, _, tokens = near_rows.shape
    size = HEAD_DIM

    def whole(row):
        return pl.BlockSpec((1, size, tokens), lambda h: (h, row, 0))

    return pl.pallas_call(
        attend_kernel,
        grid=(heads,),
        in_specs=[
            pl.BlockSpec((1, size, width), lambda h: (h, 0, place)),
            whole(1),
            whole(2),
            whole(0),
            whole(1),
        ],
        out_specs=[
            pl.BlockSpec((1, size, width), lambda h: (h, 0, 0)),
            pl.BlockSpec((1, 1, width), lambda h: (h, 0, 0)),
        ],
        out_shape=[
            jax.ShapeDtypeStruct((heads, size, width), LOW),
            jax.ShapeDtypeStruct((heads, 1, width), WIDE),
        ],
        scratch_shapes=[pltpu.VMEM((2 * tokens, size), LOW)],
        compiler_params=pltpu.CompilerParams(vmem_limit_bytes=48 * 2**20),
        cost_estimate=pl.CostEstimate(
            flops=heads * 2 * tokens * width * size * 4 * 4,
            bytes_accessed=heads * size * (width * 4 + tokens * 8),
            transcendentals=heads * 2 * tokens * width,
        ),
    )(near_rows, near_rows, near_rows, far_rows, far_rows)


def with_parts(rows, extra):
    high = extra.astype(LOW)
    rest = extra - high.astype(WIDE)
    middle = rest.astype(LOW)
    lowest = (rest - middle.astype(WIDE)).astype(LOW)
    fill = jnp.zeros((HEAD_DIM - 3, rows.shape[1]), LOW)
    return jnp.concatenate([rows, high, middle, lowest, fill], 0)


def attend_back_kernel(
    key_block, query_block,
    near_ref, far_ref, grad_ref, out_ref, stat_ref,
    grad_near_ref, grad_far_ref,
    key_rows, value_rows, key_columns, query_rows, grad_rows, query_more, grad_more, query_sum,
):
    size = HEAD_DIM
    tokens = near_ref.shape[2]
    queries = near_ref[0, :size, :] * jnp.array(size ** (-0.5), LOW)
    grads = grad_ref[0]
    ones = jnp.where(lax.broadcasted_iota(jnp.int32, (2 * tokens, size), 1) < 3, 1.0, 0.0).astype(LOW)
    key_rows[:tokens, :size] = near_ref[0, size : 2 * size, :].T
    key_rows[tokens:, :size] = far_ref[0, :size, :].T
    key_rows[:, size:] = ones
    value_rows[:tokens, :size] = near_ref[0, 2 * size :, :].T
    value_rows[tokens:, :size] = far_ref[0, size:, :].T
    value_rows[:, size:] = ones
    key_columns[:, :tokens] = near_ref[0, size : 2 * size, :]
    key_columns[:, tokens:] = far_ref[0, :size, :]
    query_rows[...] = queries.T
    grad_rows[...] = grads.T
    inner = jnp.sum(grads.astype(WIDE) * out_ref[0].astype(WIDE), 0, keepdims=True)
    query_more[...] = with_parts(queries, -stat_ref[0])
    grad_more[...] = with_parts(grads, -inner)
    query_sum[...] = jnp.zeros_like(query_sum)

    def key_step(target, key_row, value_row, base):
        def step(index, carry):
            local = pl.ds(pl.multiple_of(index * key_block, key_block), key_block)
            place = pl.ds(pl.multiple_of(base + index * key_block, key_block), key_block)
            keys, values, columns = key_rows[place, :], value_rows[place, :], key_columns[:, place]
            key_sum = jnp.zeros((key_block, size), WIDE)
            value_sum = jnp.zeros((key_block, size), WIDE)
            for part in range(tokens // query_block):
                span = slice(part * query_block, (part + 1) * query_block)
                probs = jnp.exp(jnp.dot(keys, query_more[:, span], preferred_element_type=WIDE))
                centered = jnp.dot(values, grad_more[:, span], preferred_element_type=WIDE)
                grad_scores = (probs * centered).astype(LOW)
                value_sum += jnp.dot(probs.astype(LOW), grad_rows[span, :], preferred_element_type=WIDE)
                key_sum += jnp.dot(grad_scores, query_rows[span, :], preferred_element_type=WIDE)
                query_sum[:, span] += jnp.dot(columns, grad_scores, preferred_element_type=WIDE)
            target[0, key_row : key_row + size, local] = key_sum.T.astype(LOW)
            target[0, value_row : value_row + size, local] = value_sum.T.astype(LOW)
            return carry

        lax.fori_loop(0, tokens // key_block, step, 0)

    key_step(grad_far_ref, 0, size, tokens)
    key_step(grad_near_ref, size, 2 * size, 0)
    grad_near_ref[0, :size, :] = (query_sum[...] * size ** (-0.5)).astype(LOW)


def attend_back(head, near_rows, far_rows, grads, outs, stats):
    _, _, tokens = near_rows.shape
    size = HEAD_DIM
    key_block, query_block = math.gcd(tokens, 1024), math.gcd(tokens, 512)

    def rows(count):
        return pl.BlockSpec((1, count, tokens), lambda i: (head, 0, 0))

    def result(count):
        return pl.BlockSpec((1, count, tokens), lambda i: (0, 0, 0))

    return pl.pallas_call(
        functools.partial(attend_back_kernel, key_block, query_block),
        grid=(1,),
        in_specs=[rows(3 * size), rows(2 * size), rows(size), rows(size), rows(1)],
        out_specs=[result(3 * size), result(2 * size)],
        out_shape=[
            jax.ShapeDtypeStruct((1, 3 * size, tokens), LOW),
            jax.ShapeDtypeStruct((1, 2 * size, tokens), LOW),
        ],
        scratch_shapes=[
            pltpu.VMEM((2 * tokens, 2 * size), LOW),
            pltpu.VMEM((2 * tokens, 2 * size), LOW),
            pltpu.VMEM((size, 2 * tokens), LOW),
            pltpu.VMEM((tokens, size), LOW),
            pltpu.VMEM((tokens, size), LOW),
            pltpu.VMEM((2 * size, tokens), LOW),
            pltpu.VMEM((2 * size, tokens), LOW),
            pltpu.VMEM((size, tokens), WIDE),
        ],
        compiler_params=pltpu.CompilerParams(vmem_limit_bytes=48 * 2**20),
        cost_estimate=pl.CostEstimate(
            flops=2 * tokens * tokens * size * 10 * 4,
            bytes_accessed=size * tokens * 2 * 12,
            transcendentals=2 * tokens * tokens,
        ),
    )(near_rows, far_rows, grads, outs, stats)


def reduce_weight(grad, across_tp):
    ctx_size, shard_size = lax.axis_size("ctx"), lax.axis_size("shard")
    rows = grad.shape[0] // (shard_size * ctx_size)
    low = grad.astype(LOW).reshape(shard_size, ctx_size, rows, grad.shape[1])
    core = lax.axis_index("ctx")
    mine = lax.dynamic_index_in_dim(low, core, 1, keepdims=False)
    theirs = lax.dynamic_index_in_dim(low, 1 - core, 1, keepdims=False)
    half = (mine.astype(WIDE) + swap_ctx(theirs).astype(WIDE)).astype(LOW)
    own = lax.psum_scatter(
        half.reshape(shard_size * rows, grad.shape[1]), "shard", scatter_dimension=0, tiled=True
    )
    if not across_tp:
        return own.astype(WIDE)
    count = lax.axis_size("tp")
    width = grad.shape[1] // count
    parts = scatter_list([own[:, r * width : (r + 1) * width] for r in range(count)], "tp")
    return sum(part.astype(WIDE) for part in parts)


def shards(
    latent,
    condition,
    modulator,
    modulator_bias,
    projector,
    projector_bias,
    merger,
    merger_bias,
    expander,
    expander_bias,
    reducer,
    reducer_bias,
    cotangent,
):
    tp_size, ctx_size, shard_size = (lax.axis_size(axis) for axis in ("tp", "ctx", "shard"))
    core = lax.axis_index("ctx")
    own_latent, own_cotangent = latent[0], cotangent[0]
    block, model_width = own_latent.shape
    local_width = projector.shape[2]
    heads = local_width // HEAD_DIM
    local_hidden = expander.shape[1]
    kept_rows = projector.shape[0]

    latent_blocks = gather_list(own_latent, "tp")

    conditions = lax.all_gather(condition, "shard", axis=0, tiled=True)
    scaled_all = silu_gate(conditions.astype(WIDE)).astype(LOW)
    place = lax.axis_index("shard") * kept_rows
    terms = jnp.dot(
        lax.dynamic_slice_in_dim(scaled_all, place, kept_rows, 1),
        modulator,
        preferred_element_type=WIDE,
    )
    terms = lax.all_to_all(terms, "shard", 0, 0, tiled=True)
    modulation = jnp.sum(terms, 0, keepdims=True) + modulator_bias.astype(WIDE)
    settings = [
        modulation[:, index * model_width : (index + 1) * model_width] for index in range(6)
    ]
    shift_one, scale_one, gate_one, shift_two, scale_two, gate_two = settings

    own_projector = (
        projector.reshape(kept_rows, 3, heads, HEAD_DIM)
        .transpose(2, 1, 3, 0)
        .reshape(3 * local_width, kept_rows)
    )
    head_projector = lax.all_gather(own_projector, "shard", axis=1, tiled=True)
    zero_bias = jnp.zeros((1, local_width), projector_bias.dtype)
    qkv_bias = (
        jnp.concatenate([projector_bias[:1], zero_bias, projector_bias[1:]], 0)
        .reshape(3, heads, HEAD_DIM)
        .transpose(1, 0, 2)
        .reshape(3 * local_width, 1)
        .astype(WIDE)
    )

    normed_rows = jnp.concatenate(
        [modulate(rows.astype(WIDE), scale_one, shift_one).astype(LOW) for rows in latent_blocks], 0
    )
    tokens = normed_rows.shape[0]
    projected = (dot_wide(head_projector, normed_rows, 1, 1) + qkv_bias).astype(LOW)
    near_rows = projected.reshape(heads, 3 * HEAD_DIM, tokens)
    far_rows = swap_ctx(near_rows[:, HEAD_DIM:, :])

    half_hidden = local_hidden // ctx_size
    expander_half = lax.dynamic_slice_in_dim(expander, core * half_hidden, half_hidden, 1)
    reducer_half = lax.dynamic_slice_in_dim(reducer, core * half_hidden, half_hidden, 0).T
    pieces = jnp.concatenate([expander_half, reducer_half], 1)
    pieces = after(pieces, latent_blocks[1], latent_blocks[2 % tp_size], latent_blocks[3 % tp_size])
    pieces = jnp.stack(gather_list(pieces, "tp"))
    pieces = lax.all_gather(pieces, "shard", axis=1, tiled=True)
    other = swap_ctx(pieces)
    first, second = jnp.where(core == 0, pieces, other), jnp.where(core == 0, other, pieces)
    full_expander = jnp.concatenate(
        [part[r, :, :half_hidden] for r in range(tp_size) for part in (first, second)], 1
    )
    full_reducer = jnp.concatenate(
        [part[r, :, half_hidden:] for r in range(tp_size) for part in (first, second)], 1
    )
    merger_pieces = jnp.stack(gather_list(merger.T, "tp"))
    merger_pieces = lax.all_gather(merger_pieces, "shard", axis=1, tiled=True)
    full_merger = jnp.concatenate([merger_pieces[r] for r in range(tp_size)], 1)
    full_expander_bias = jnp.concatenate(gather_list(expander_bias, "tp")).astype(WIDE)

    outs, stats, sent = [None] * tp_size, [None] * tp_size, [None] * tp_size
    order = sorted(range(tp_size), key=lambda r: -min(r, tp_size - r))
    for r in order:
        outs[r], stats[r] = attend(near_rows, far_rows, r, block)
        sent[r] = outs[r].reshape(local_width, block)
    attended = jnp.concatenate(scatter_list(sent, "tp"), 0)
    all_outs, all_stats = jnp.concatenate(outs, 2), jnp.concatenate(stats, 2)

    latent_wide = own_latent.astype(WIDE)
    branch = dot_wide(attended, full_merger, 0, 1) + merger_bias.astype(WIDE)
    middle = latent_wide + gate_one * branch
    normed_two_wide, norm_back_two = jax.vjp(modulate, middle, scale_two, shift_two)
    normed_two = normed_two_wide.astype(LOW)
    hidden = dot_wide(normed_two, full_expander, 1, 0) + full_expander_bias
    activated, gelu_back = jax.vjp(gelu_tanh, hidden)
    activated_low = activated.astype(LOW)
    feed = dot_wide(activated_low, full_reducer, 1, 1) + reducer_bias.astype(WIDE)
    block_output = (middle + gate_two * feed).astype(LOW)
    grad_output = own_cotangent.astype(WIDE)
    grad_feed = (gate_two * grad_output).astype(LOW)
    grad_gate_two = jnp.sum(grad_output * feed, 0, keepdims=True)
    grad_activated = dot_wide(grad_feed, full_reducer, 1, 0)
    grad_hidden = gelu_back(grad_activated)[0].astype(LOW)
    grad_normed_two = dot_wide(grad_hidden, full_expander, 1, 1)
    grad_middle_norm, grad_scale_two, grad_shift_two = norm_back_two(grad_normed_two)
    grad_middle = grad_output + grad_middle_norm
    grad_gate_one = jnp.sum(grad_middle * branch, 0, keepdims=True)
    grad_branch = (gate_one * grad_middle).astype(LOW)
    grad_attended = dot_wide(full_merger, grad_branch, 0, 1).astype(LOW)
    grad_blocks = scatter_list(
        [grad_attended[r * local_width : (r + 1) * local_width] for r in range(tp_size)], "tp"
    )
    all_grads = jnp.concatenate(grad_blocks, 1).reshape(heads, HEAD_DIM, tokens)

    grad_reducer = reduce_weight(dot_wide(grad_feed, activated_low, 0, 0), True).T
    grad_expander = reduce_weight(dot_wide(normed_two, grad_hidden, 0, 0), True)
    grad_merger = reduce_weight(dot_wide(grad_branch, attended, 0, 1), True).T

    tail_projector = after(head_projector, all_outs)
    full_projector = jnp.concatenate(gather_list(tail_projector, "tp"), 0).reshape(
        tp_size, heads, 3 * HEAD_DIM, model_width
    )
    head_grads, grad_normed = [], 0.0
    for head in range(heads):
        near, far = attend_back(head, near_rows, far_rows, all_grads, all_outs, all_stats)
        shared = near[0, HEAD_DIM:].astype(WIDE) + swap_ctx(far[0]).astype(WIDE)
        rows = jnp.concatenate([near[0, :HEAD_DIM], shared.astype(LOW)], 0)
        head_grads.append(rows)
        arrived = scatter_list([rows[:, r * block : (r + 1) * block] for r in range(tp_size)], "tp")
        grad_normed = grad_normed + dot_wide(
            jnp.concatenate(arrived, 0),
            full_projector[:, head].reshape(tp_size * 3 * HEAD_DIM, model_width),
            0,
            0,
        )
    qkv_grads = jnp.concatenate(head_grads, 0)
    grad_projector = reduce_weight(dot_wide(normed_rows, qkv_grads, 0, 1), False)
    grad_projector = (
        grad_projector.reshape(-1, heads, 3, HEAD_DIM).transpose(0, 2, 1, 3).reshape(-1, 3, local_width)
    )
    _, norm_back = jax.vjp(modulate, latent_wide, scale_one, shift_one)
    grad_latent_norm, grad_scale_one, grad_shift_one = norm_back(grad_normed)
    grad_latent = grad_middle + grad_latent_norm

    token_bias = jnp.concatenate(
        [
            jnp.sum(grad_feed, 0, keepdims=True, dtype=WIDE),
            jnp.sum(grad_branch, 0, keepdims=True, dtype=WIDE),
        ],
        0,
    )
    token_bias = sum_over(token_bias, ("ctx", "tp", "shard"))
    hidden_bias = jnp.sum(grad_hidden, 0, dtype=WIDE).reshape(tp_size, 1, local_hidden)
    hidden_bias = sum(
        part
        for part in [
            hidden_bias[0],
            *(
                lax.ppermute(
                    hidden_bias[r], "tp", [(i, (i + r) % tp_size) for i in range(tp_size)]
                )
                for r in range(1, tp_size)
            ),
        ]
    )
    hidden_bias = sum_over(hidden_bias, ("ctx", "shard"))[0]
    column_sums = jnp.sum(qkv_grads, 1, dtype=WIDE).reshape(heads, 3, HEAD_DIM)
    projector_sums = sum_over(
        jnp.stack([column_sums[:, 0].reshape(-1), column_sums[:, 2].reshape(-1)]), ("ctx", "shard")
    )

    own_settings = jnp.concatenate(
        [
            grad_shift_one,
            grad_scale_one,
            grad_gate_one,
            grad_shift_two,
            grad_scale_two,
            grad_gate_two,
        ],
        1,
    )
    own_settings = sum_over(own_settings, ("ctx", "tp"))
    all_settings = lax.all_gather(own_settings, "shard", axis=0, tiled=True)
    gate_terms = lax.dot_general(
        all_settings, modulator.astype(WIDE), (((1,), (1,)), ((), ())), precision=PRECISE
    )
    gate_terms = lax.all_to_all(gate_terms, "shard", 0, 1, tiled=True)
    _, silu_back = jax.vjp(silu_gate, condition.astype(WIDE))
    grad_condition = silu_back(gate_terms)[0]
    column_count = all_settings.shape[1] // tp_size
    tp_settings = lax.dynamic_slice_in_dim(
        all_settings, lax.axis_index("tp") * column_count, column_count, 1
    )
    row_count = kept_rows // ctx_size
    tp_scaled = lax.dynamic_slice_in_dim(
        scaled_all.astype(WIDE), place + core * row_count, row_count, 1
    )
    grad_modulator = lax.dot_general(
        tp_scaled, tp_settings, (((0,), (0,)), ((), ())), precision=PRECISE
    )
    grad_modulator_bias = jnp.sum(tp_settings, 0)
    return (
        block_output[None],
        grad_latent[None],
        grad_condition,
        grad_modulator,
        grad_modulator_bias,
        grad_projector,
        projector_sums,
        grad_merger,
        token_bias[1],
        grad_expander,
        hidden_bias,
        grad_reducer,
        token_bias[0],
    )


def solution(mesh):
    in_specs = (
        P("shard", ("ctx", "tp"), None),
        P("shard", None),
        P("shard", None),
        P(),
        P("shard", None, "tp"),
        P(None, "tp"),
        P("tp", "shard"),
        P(),
        P("shard", "tp"),
        P("tp"),
        P("tp", "shard"),
        P(),
        P("shard", ("ctx", "tp"), None),
    )
    out_specs = (
        P("shard", ("ctx", "tp"), None),
        P("shard", ("ctx", "tp"), None),
        P("shard", None),
        P(("shard", "ctx"), "tp"),
        P("tp"),
        P(("shard", "ctx"), None, "tp"),
        P(None, "tp"),
        P("tp", ("shard", "ctx")),
        P(),
        P(("shard", "ctx"), "tp"),
        P("tp"),
        P("tp", ("shard", "ctx")),
        P(),
    )
    return jax.shard_map(shards, mesh=mesh, in_specs=in_specs, out_specs=out_specs, check_vma=False)
```

```python
import functools
import math

import jax
import jax.numpy as jnp
from jax import lax
from jax.experimental import pallas as pl
from jax.experimental.pallas import tpu as pltpu
from jax.sharding import PartitionSpec as P

HEAD_DIM = 64
PRECISE = lax.Precision.HIGHEST
LOW = jnp.bfloat16
WIDE = jnp.float32


def layer_norm(values):
    row_mean = jnp.mean(values, -1, keepdims=True)
    centered = values - row_mean
    variance = jnp.mean(centered * centered, -1, keepdims=True)
    return centered * lax.rsqrt(variance + 1e-06)


def gelu_tanh(values):
    return (
        0.5
        * values
        * (1.0 + jnp.tanh(0.7978845608028654 * (values + 0.044715 * values * values * values)))
    )


def silu_gate(values):
    return values * jax.nn.sigmoid(values)


def modulate(values, scale_part, shift_part):
    return layer_norm(values) * (1.0 + scale_part) + shift_part


def dot_wide(left, right, left_dim, right_dim):
    return lax.dot_general(
        left, right, (((left_dim,), (right_dim,)), ((), ())), preferred_element_type=WIDE
    )


def gather_list(block, axis):
    count = lax.axis_size(axis)
    return [block] + [
        lax.ppermute(block, axis, [(i, (i - r) % count) for i in range(count)])
        for r in range(1, count)
    ]


def scatter_list(blocks, axis):
    count = lax.axis_size(axis)
    arrived = {
        (count - r) % count: lax.ppermute(
            blocks[r], axis, [(i, (i + r) % count) for i in range(count)]
        )
        for r in range(1, count)
    }
    arrived[0] = blocks[0]
    return [arrived[r] for r in range(count)]


def swap_ctx(block):
    count = lax.axis_size("ctx")
    return lax.ppermute(block, "ctx", [(i, (i + 1) % count) for i in range(count)])


def sum_over(value, axes):
    for axis in axes:
        step = 1
        while step < lax.axis_size(axis):
            value = value + lax.ppermute(
                value, axis, [(i, i ^ step) for i in range(lax.axis_size(axis))]
            )
            step *= 2
    return value


def rotated(rows, start):
    return lax.dynamic_slice_in_dim(jnp.concatenate([rows, rows], 0), start, rows.shape[0], 0)


def mirror(block, r):
    return lax.ppermute(block, "shard", [(i, i ^ r) for i in range(lax.axis_size("shard"))])


def mirror_gather(block):
    return [block] + [mirror(block, r) for r in range(1, lax.axis_size("shard"))]


def mirror_exchange(blocks):
    return [blocks[0]] + [mirror(block, r) for r, block in enumerate(blocks) if r > 0]


def in_shard_order(blocks):
    own, bit = lax.axis_index("shard"), 1
    while bit < len(blocks):
        flip = (own & bit) != 0
        blocks = [jnp.where(flip, blocks[j ^ bit], blocks[j]) for j in range(len(blocks))]
        bit *= 2
    return blocks


def tree_sum(blocks):
    while len(blocks) > 1:
        blocks = [blocks[i] + blocks[i + 1] for i in range(0, len(blocks), 2)]
    return blocks[0]


def ordered_call(kernel, operands, in_specs, out_specs, out_shape, before=(), through=(), **rest):
    count, through_count, results = len(operands), len(through), len(out_specs)
    extra = through_count + len(before)
    unread = pl.BlockSpec(memory_space=pl.ANY)

    def body(*refs):
        after_inputs = refs[count + extra :]
        kernel(*refs[:count], *after_inputs[:results], *after_inputs[results + through_count :])

    made = pl.pallas_call(
        body,
        in_specs=list(in_specs) + [unread] * extra,
        out_specs=list(out_specs) + [unread] * through_count,
        out_shape=list(out_shape) + [jax.ShapeDtypeStruct(x.shape, x.dtype) for x in through],
        input_output_aliases={count + i: results + i for i in range(through_count)},
        **rest,
    )(*operands, *through, *before)
    return made[:results], made[results:]


def tie(values, *before):
    return ordered_call(
        lambda *refs: None,
        (),
        (),
        (),
        (),
        before,
        values,
        cost_estimate=pl.CostEstimate(flops=1, bytes_accessed=1, transcendentals=0),
    )[1]


def attend_kernel(query_ref, key_ref, value_ref, far_key_ref, far_value_ref, out_ref, stat_ref, key_rows):
    near = key_ref.shape[2]
    key_rows[:near, :] = key_ref[0].T
    key_rows[near:, :] = far_key_ref[0].T
    queries = query_ref[0] * jnp.array(HEAD_DIM ** (-0.5), LOW)
    columns = queries.shape[1]
    top = total = mixed = None
    for half, values in enumerate((value_ref, far_value_ref)):
        scores = jnp.dot(
            key_rows[half * near : (half + 1) * near, :], queries, preferred_element_type=WIDE
        )
        block_top = jnp.max(scores, 0, keepdims=True)
        new_top = block_top if top is None else jnp.maximum(top, block_top)
        exponent = jnp.exp(scores - new_top)
        block_total = jnp.sum(exponent, 0, keepdims=True)
        block_mixed = jnp.dot(values[0], exponent.astype(LOW), preferred_element_type=WIDE)
        if top is None:
            total, mixed = block_total, block_mixed
        else:
            fade = jnp.exp(top - new_top)
            total = total * fade + block_total
            mixed = mixed * fade + block_mixed
        top = new_top
    out_ref[0] = (mixed / total).astype(LOW)
    stat_ref[0] = top + jnp.log(total)


def attend(near_rows, far_rows, place, width, before=(), through=()):
    heads, _, tokens = near_rows.shape
    size = HEAD_DIM

    def whole(row):
        return pl.BlockSpec((1, size, tokens), lambda h: (h, row, 0))

    return ordered_call(
        attend_kernel,
        (near_rows, near_rows, near_rows, far_rows, far_rows),
        grid=(heads,),
        in_specs=[
            pl.BlockSpec((1, size, width), lambda h: (h, 0, place)),
            whole(1),
            whole(2),
            whole(0),
            whole(1),
        ],
        out_specs=[
            pl.BlockSpec((1, size, width), lambda h: (h, 0, 0)),
            pl.BlockSpec((1, 1, width), lambda h: (h, 0, 0)),
        ],
        out_shape=[
            jax.ShapeDtypeStruct((heads, size, width), LOW),
            jax.ShapeDtypeStruct((heads, 1, width), WIDE),
        ],
        scratch_shapes=[pltpu.VMEM((2 * tokens, size), LOW)],
        compiler_params=pltpu.CompilerParams(vmem_limit_bytes=48 * 2**20),
        cost_estimate=pl.CostEstimate(
            flops=heads * 2 * tokens * width * size * 4 * 4,
            bytes_accessed=heads * size * (width * 4 + tokens * 8),
            transcendentals=heads * 2 * tokens * width,
        ),
        before=before,
        through=through,
    )


def with_parts(rows, extra):
    high = extra.astype(LOW)
    rest = extra - high.astype(WIDE)
    middle = rest.astype(LOW)
    lowest = (rest - middle.astype(WIDE)).astype(LOW)
    fill = jnp.zeros((HEAD_DIM - 3, rows.shape[1]), LOW)
    return jnp.concatenate([rows, high, middle, lowest, fill], 0)


def attend_back_kernel(
    key_block, query_block, first,
    query_ref, key_ref, value_ref, grad_ref, out_ref, stat_ref, sum_ref,
    grad_query_ref, grad_pair_ref,
    key_rows, value_rows, query_rows, grad_rows, query_more, grad_more, query_sum,
):
    size = HEAD_DIM
    tokens = query_ref.shape[2]
    keys_held = key_ref.shape[2]
    queries = query_ref[0] * jnp.array(size ** (-0.5), LOW)
    grads = grad_ref[0]
    ones = jnp.where(lax.broadcasted_iota(jnp.int32, (keys_held, size), 1) < 3, 1.0, 0.0).astype(LOW)
    key_rows[:, :size] = key_ref[0].T
    key_rows[:, size:] = ones
    value_rows[:, :size] = value_ref[0].T
    value_rows[:, size:] = ones
    query_rows[...] = queries.T
    grad_rows[...] = grads.T
    inner = jnp.sum(grads.astype(WIDE) * out_ref[0].astype(WIDE), 0, keepdims=True)
    query_more[...] = with_parts(queries, -stat_ref[0])
    grad_more[...] = with_parts(grads, -inner)
    query_sum[...] = jnp.zeros_like(query_sum) if first else sum_ref[0]

    def step(index, carry):
        place = pl.ds(pl.multiple_of(index * key_block, key_block), key_block)
        keys, values, columns = key_rows[place, :], value_rows[place, :], key_ref[0, :, place]
        key_sum = jnp.zeros((key_block, size), WIDE)
        value_sum = jnp.zeros((key_block, size), WIDE)
        for part in range(tokens // query_block):
            span = slice(part * query_block, (part + 1) * query_block)
            probs = jnp.exp(jnp.dot(keys, query_more[:, span], preferred_element_type=WIDE))
            centered = jnp.dot(values, grad_more[:, span], preferred_element_type=WIDE)
            grad_scores = (probs * centered).astype(LOW)
            value_sum += jnp.dot(probs.astype(LOW), grad_rows[span, :], preferred_element_type=WIDE)
            key_sum += jnp.dot(grad_scores, query_rows[span, :], preferred_element_type=WIDE)
            query_sum[:, span] += jnp.dot(columns, grad_scores, preferred_element_type=WIDE)
        grad_pair_ref[0, :size, place] = key_sum.T.astype(LOW)
        grad_pair_ref[0, size:, place] = value_sum.T.astype(LOW)
        return carry

    lax.fori_loop(0, keys_held // key_block, step, 0)
    if first:
        grad_query_ref[0] = query_sum[...]
    else:
        grad_query_ref[0] = (query_sum[...] * size ** (-0.5)).astype(LOW)


def attend_back(head, near_rows, pair_rows, key_place, grads, outs, stats, query_sum, before=(), through=()):
    tokens = near_rows.shape[2]
    size = HEAD_DIM
    key_block, query_block = math.gcd(tokens, 1024), math.gcd(tokens, 512)
    first = query_sum is None
    if first:
        query_sum = jnp.zeros((1, 8, 128), WIDE)

    def rows(count, place=0):
        return pl.BlockSpec((1, count, tokens), lambda i: (head, place, 0))

    def result(count):
        return pl.BlockSpec((1, count, tokens), lambda i: (0, 0, 0))

    return ordered_call(
        functools.partial(attend_back_kernel, key_block, query_block, first),
        (near_rows, pair_rows, pair_rows, grads, outs, stats, query_sum),
        grid=(1,),
        in_specs=[
            rows(size),
            rows(size, key_place),
            rows(size, key_place + 1),
            rows(size),
            rows(size),
            rows(1),
            pl.BlockSpec(query_sum.shape, lambda i: (0, 0, 0)),
        ],
        out_specs=[result(size), result(2 * size)],
        out_shape=[
            jax.ShapeDtypeStruct((1, size, tokens), WIDE if first else LOW),
            jax.ShapeDtypeStruct((1, 2 * size, tokens), LOW),
        ],
        scratch_shapes=[
            pltpu.VMEM((tokens, 2 * size), LOW),
            pltpu.VMEM((tokens, 2 * size), LOW),
            pltpu.VMEM((tokens, size), LOW),
            pltpu.VMEM((tokens, size), LOW),
            pltpu.VMEM((2 * size, tokens), LOW),
            pltpu.VMEM((2 * size, tokens), LOW),
            pltpu.VMEM((size, tokens), WIDE),
        ],
        compiler_params=pltpu.CompilerParams(vmem_limit_bytes=48 * 2**20),
        cost_estimate=pl.CostEstimate(
            flops=tokens * tokens * size * 10 * 4,
            bytes_accessed=size * tokens * 2 * 9,
            transcendentals=tokens * tokens,
        ),
        before=before,
        through=through,
    )


def weight_kernel(
    normed_ref, hidden_ref, far_hidden_ref, feed_ref, active_ref, far_active_ref, branch_ref, heads_ref,
    expander_ref, far_expander_ref, reducer_ref, far_reducer_ref, merger_ref,
    normed_columns, feed_columns, branch_columns,
):
    @pl.when(pl.program_id(0) == 0)
    def _():
        normed_columns[...] = normed_ref[...].T
        feed_columns[...] = feed_ref[...].T
        branch_columns[...] = branch_ref[...].T

    def product(left, right):
        return jnp.dot(left, right, preferred_element_type=WIDE).astype(LOW)

    expander_ref[...] = product(normed_columns[...], hidden_ref[...])
    far_expander_ref[...] = product(normed_columns[...], far_hidden_ref[...])
    reducer_ref[...] = product(feed_columns[...], active_ref[...])
    far_reducer_ref[...] = product(feed_columns[...], far_active_ref[...])
    count = merger_ref.shape[0]
    place = pl.ds(pl.multiple_of(pl.program_id(0) * count, count), count)
    merger_ref[...] = dot_wide(branch_columns[place, :], heads_ref[...], 1, 1).astype(LOW)


def weight_terms(normed, grad_hidden, grad_feed, activated, grad_branch, attended, steps, before):
    tokens, width = normed.shape
    share = grad_hidden[0].shape[1]

    def whole(array):
        return pl.BlockSpec(array.shape, lambda i: (0, 0))

    units = pl.BlockSpec((tokens, share // steps), lambda i: (0, i))
    made = pl.BlockSpec((width, share // steps), lambda i: (0, i))
    operands = (normed, *grad_hidden, grad_feed, *activated, grad_branch, attended)
    return ordered_call(
        weight_kernel,
        operands,
        grid=(steps,),
        in_specs=[whole(normed), units, units, whole(grad_feed), units, units]
        + [whole(grad_branch), whole(attended)],
        out_specs=[made] * 4 + [pl.BlockSpec((width // steps, attended.shape[0]), lambda i: (i, 0))],
        out_shape=[jax.ShapeDtypeStruct((width, share), LOW)] * 4
        + [jax.ShapeDtypeStruct((width, attended.shape[0]), LOW)],
        scratch_shapes=[pltpu.VMEM((width, tokens), LOW)] * 3,
        compiler_params=pltpu.CompilerParams(vmem_limit_bytes=48 * 2**20),
        cost_estimate=pl.CostEstimate(
            flops=2 * tokens * width * (4 * share + width), bytes_accessed=2**25, transcendentals=0
        ),
        before=before,
    )[0]


def core_half(grad):
    ctx_size, shard_size = lax.axis_size("ctx"), lax.axis_size("shard")
    rows = grad.shape[0] // (shard_size * ctx_size)
    low = grad.astype(LOW).reshape(shard_size, ctx_size, rows, grad.shape[1])
    core = lax.axis_index("ctx")
    mine = lax.dynamic_index_in_dim(low, core, 1, keepdims=False)
    theirs = lax.dynamic_index_in_dim(low, 1 - core, 1, keepdims=False)
    return (
        mine.reshape(shard_size * rows, grad.shape[1]),
        theirs.reshape(shard_size * rows, grad.shape[1]),
    )


def sum_low(left, right):
    return (left.astype(WIDE) + right.astype(WIDE)).astype(LOW)


def shards(
    latent,
    condition,
    modulator,
    modulator_bias,
    projector,
    projector_bias,
    merger,
    merger_bias,
    expander,
    expander_bias,
    reducer,
    reducer_bias,
    cotangent,
):
    tp_size, ctx_size, shard_size = (lax.axis_size(axis) for axis in ("tp", "ctx", "shard"))
    core = lax.axis_index("ctx")
    own_latent, own_cotangent = latent[0], cotangent[0]
    block, model_width = own_latent.shape
    local_width = projector.shape[2]
    heads = local_width // HEAD_DIM
    head_columns = 3 * HEAD_DIM
    local_hidden = expander.shape[1]
    half_hidden = local_hidden // ctx_size
    kept_rows = projector.shape[0]
    place = lax.axis_index("shard") * kept_rows

    conditions = jnp.concatenate(mirror_gather(condition.astype(WIDE)), 0)
    def half_units(weight, axis):
        return lax.dynamic_slice_in_dim(weight, core * half_hidden, half_hidden, axis)

    share = tp_size * half_hidden
    latent_blocks = gather_list(own_latent, "tp")
    own_reducer = lax.all_gather(
        jnp.concatenate(gather_list(half_units(reducer, 0).T, "tp"), 1), "shard", axis=0, tiled=True
    )

    scaled_all = silu_gate(conditions).astype(LOW)
    terms = jnp.dot(
        lax.dynamic_slice_in_dim(scaled_all, place, kept_rows, 1),
        modulator,
        preferred_element_type=WIDE,
    )
    terms = mirror_exchange([terms[r : r + 1] for r in range(shard_size)])
    modulation = tree_sum(terms) + modulator_bias.astype(WIDE)

    own_projector = (
        projector.reshape(kept_rows, 3, heads, HEAD_DIM)
        .transpose(0, 2, 1, 3)
        .reshape(kept_rows, 3 * local_width)
    )
    head_projector = jnp.concatenate(in_shard_order(mirror_gather(own_projector)), 0)
    zero_bias = jnp.zeros((1, local_width), projector_bias.dtype)
    qkv_bias = (
        jnp.concatenate([projector_bias[:1], zero_bias, projector_bias[1:]], 0)
        .reshape(3, heads, HEAD_DIM)
        .transpose(1, 0, 2)
        .reshape(3 * local_width, 1)
        .astype(WIDE)
    )
    settings = [
        modulation[:, index * model_width : (index + 1) * model_width] for index in range(6)
    ]
    shift_one, scale_one, gate_one, shift_two, scale_two, gate_two = settings

    latent_blocks = [latent_blocks[0], *tie(latent_blocks[1:], head_projector, modulation)]
    normed_rows = jnp.concatenate(
        [modulate(rows.astype(WIDE), scale_one, shift_one).astype(LOW) for rows in latent_blocks], 0
    )
    tokens = normed_rows.shape[0]
    projected = (dot_wide(head_projector, normed_rows, 0, 1) + qkv_bias).astype(LOW)
    near_rows = projected.reshape(heads, head_columns, tokens)
    far_rows = swap_ctx(near_rows[:, HEAD_DIM:, :])

    bias_rows = jnp.zeros((16, half_hidden + local_width), expander_bias.dtype)
    for index, part in enumerate((core, 1 - core)):
        half_bias = lax.dynamic_slice_in_dim(expander_bias, part * half_hidden, half_hidden, 0)
        bias_rows = bias_rows.at[index, :half_hidden].set(half_bias)
    pieces = jnp.concatenate([half_units(expander, 1), merger.T], 1)
    pieces = jnp.concatenate([pieces, bias_rows], 0)
    pieces = gather_list(tie([pieces], *latent_blocks[1:])[0], "tp")
    pieces = tie(pieces, near_rows)
    own_expander = lax.all_gather(
        jnp.concatenate([piece[:kept_rows, :half_hidden] for piece in pieces], 1),
        "shard",
        axis=0,
        tiled=True,
    )
    full_merger = lax.all_gather(
        jnp.concatenate([piece[:kept_rows, half_hidden:] for piece in pieces], 1),
        "shard",
        axis=0,
        tiled=True,
    )
    part_biases = [
        jnp.concatenate(
            [piece[kept_rows + index : kept_rows + index + 1, :half_hidden] for piece in pieces], 1
        )
        for index in range(2)
    ]
    outs, stats, sent = [None] * tp_size, [None] * tp_size, [None] * tp_size
    order = sorted(range(tp_size), key=lambda r: -min(r, tp_size - r))
    previous = ()
    for r in order:
        (outs[r], stats[r]), _ = attend(near_rows, far_rows, r, block, previous)
        sent[r] = outs[r].reshape(local_width, block)
        previous = (outs[r],)
    attended = jnp.concatenate(scatter_list(sent, "tp"), 0)
    all_outs, all_stats = jnp.concatenate(outs, 2), jnp.concatenate(stats, 2)

    own_expander, full_merger = tie([own_expander, full_merger], outs[order[-1]])
    expanders = [own_expander, swap_ctx(own_expander)]
    reducers = [own_reducer, swap_ctx(own_reducer)]
    core_width = model_width // ctx_size
    tail_projector = lax.dynamic_slice_in_dim(head_projector, core * core_width, core_width, 0).T
    projectors = lax.all_gather(
        tie([tail_projector], outs[order[-1]])[0], "tp", axis=0, tiled=True
    )
    latent_wide = own_latent.astype(WIDE)
    branch = dot_wide(attended, full_merger, 0, 1) + merger_bias.astype(WIDE)
    middle = latent_wide + gate_one * branch
    normed_two_wide, norm_back_two = jax.vjp(modulate, middle, scale_two, shift_two)
    normed_two = normed_two_wide.astype(LOW)
    grad_output = own_cotangent.astype(WIDE)
    grad_feed = (gate_two * grad_output).astype(LOW)
    feed, grad_normed_two = reducer_bias.astype(WIDE), 0.0
    activated, grad_hidden = [], []
    for full_expander, full_reducer, part_bias in zip(expanders, reducers, part_biases):
        hidden = dot_wide(normed_two, full_expander, 1, 0) + part_bias.astype(WIDE)
        active, gelu_back = jax.vjp(gelu_tanh, hidden)
        activated.append(active.astype(LOW))
        feed = feed + dot_wide(activated[-1], full_reducer, 1, 1)
        grad_hidden.append(gelu_back(dot_wide(grad_feed, full_reducer, 1, 0))[0].astype(LOW))
        grad_normed_two = grad_normed_two + dot_wide(grad_hidden[-1], full_expander, 1, 1)
    block_output = (middle + gate_two * feed).astype(LOW)
    grad_gate_two = jnp.sum(grad_output * feed, 0, keepdims=True)
    grad_middle_norm, grad_scale_two, grad_shift_two = norm_back_two(grad_normed_two)
    grad_middle = grad_output + grad_middle_norm
    grad_gate_one = jnp.sum(grad_middle * branch, 0, keepdims=True)
    grad_branch = (gate_one * grad_middle).astype(LOW)
    grad_attended = dot_wide(full_merger, grad_branch, 0, 1).astype(LOW)
    grad_blocks = scatter_list(
        [grad_attended[r * local_width : (r + 1) * local_width] for r in range(tp_size)], "tp"
    )

    weight_parts = weight_terms(
        normed_two, grad_hidden, grad_feed, activated, grad_branch, attended, tp_size, (grad_attended,)
    )
    grad_blocks = tie(grad_blocks, *weight_parts)
    all_grads = jnp.concatenate(grad_blocks, 1).reshape(heads, HEAD_DIM, tokens)

    def in_order(left, right, axis):
        return jnp.where(
            core == 0, jnp.concatenate([left, right], axis), jnp.concatenate([right, left], axis)
        )

    tp_turn = lax.rem(tp_size - lax.axis_index("tp"), tp_size)
    hidden_sums = in_order(
        *(jnp.sum(part, 0, dtype=WIDE).reshape(tp_size, half_hidden) for part in grad_hidden), 1
    )
    early_sums = jnp.concatenate(
        [
            grad_gate_one,
            grad_shift_two,
            grad_scale_two,
            grad_gate_two,
            jnp.sum(grad_feed, 0, keepdims=True, dtype=WIDE),
            jnp.sum(grad_branch, 0, keepdims=True, dtype=WIDE),
            rotated(hidden_sums, tp_turn),
        ],
        0,
    )

    def projector_half(rows):
        own, other = core_half(dot_wide(normed_rows, jnp.concatenate(rows, 0), 0, 1))
        return sum_low(own, swap_ctx(other))

    head_rows, arrived_rows = [], []
    for head in range(heads):
        before = ()
        if head == 1:
            before = (head_rows[0],)
        elif head == 2:
            before = (head_rows[1], *arrived_rows[0])
        (partial, far), _ = attend_back(
            head, near_rows, far_rows, 0, all_grads, all_outs, all_stats, None, before
        )
        before = ()
        if head == 0:
            came = tie([swap_ctx(weight_parts[i]) for i in (1, 3, 4)], partial)
            weight_halves = [sum_low(weight_parts[2 * i], came[i]) for i in range(3)]
            weight_sums = [
                lax.psum_scatter(half, "shard", scatter_dimension=0, tiled=True)
                for half in weight_halves
            ]
            before = tuple(weight_halves)
        elif head == 1:
            projectors = tie([projectors], partial)[0]
            other_projectors = swap_ctx(projectors)
        elif head == 2:
            early_projector = projector_half(head_rows)
            before = (other_projectors, *arrived_rows[1], early_projector)
        far_came = swap_ctx(far[0])
        (grad_query, near), _ = attend_back(
            head, near_rows, near_rows, 1, all_grads, all_outs, all_stats, partial, before
        )
        rows = jnp.concatenate([grad_query[0], sum_low(near[0], far_came)], 0)
        head_rows.append(rows)
        arrived_rows.append(
            scatter_list([rows[:, r * block : (r + 1) * block] for r in range(tp_size)], "tp")
        )
    rows = jnp.zeros((tp_size * heads * head_columns, block), LOW)
    for head, arrived in enumerate(arrived_rows):
        for r, part in enumerate(arrived):
            turn = lax.rem(lax.axis_index("tp") + r, tp_size)
            rows = lax.dynamic_update_slice_in_dim(
                rows, part, (turn * heads + head) * head_columns, 0
            )
    grad_normed = in_order(
        *(dot_wide(rows, part, 0, 0) for part in (projectors, other_projectors)), 1
    )
    _, norm_back = jax.vjp(modulate, latent_wide, scale_one, shift_one)
    grad_latent_norm, grad_scale_one, grad_shift_one = norm_back(grad_normed)
    grad_latent = grad_middle + grad_latent_norm

    def from_peers(columns):
        width = columns.shape[1] // tp_size
        parts = scatter_list([columns[:, r * width : (r + 1) * width] for r in range(tp_size)], "tp")
        return sum(part.astype(WIDE) for part in parts)

    row_count = kept_rows // ctx_size
    summed = from_peers(
        tie(
            [
                jnp.concatenate(
                    [
                        part[:, r * (part.shape[1] // tp_size) : (r + 1) * (part.shape[1] // tp_size)]
                        for r in range(tp_size)
                        for part in weight_sums
                    ],
                    1,
                )
            ],
            *arrived_rows[-1],
        )[0]
    )
    two = summed[:, : 2 * half_hidden]
    own_two = lax.dynamic_slice_in_dim(two, core * row_count, row_count, 0)
    other_two = swap_ctx(lax.dynamic_slice_in_dim(two, (1 - core) * row_count, row_count, 0))
    grad_expander = in_order(own_two[:, :half_hidden], other_two[:, :half_hidden], 1)
    grad_reducer = in_order(own_two[:, half_hidden:], other_two[:, half_hidden:], 1).T
    grad_merger = lax.dynamic_slice_in_dim(summed[:, 2 * half_hidden :], core * row_count, row_count, 0).T

    column_sums = jnp.sum(jnp.concatenate(head_rows, 0), 1, dtype=WIDE).reshape(heads, 3, HEAD_DIM)
    bias_sums = jnp.stack([column_sums[:, 0].reshape(-1), column_sums[:, 2].reshape(-1)])
    bias_sums = lax.dynamic_update_slice_in_dim(
        jnp.zeros((2, model_width), WIDE), bias_sums, lax.axis_index("tp") * local_width, 1
    )
    sums = jnp.concatenate([grad_shift_one, grad_scale_one, early_sums, bias_sums], 0)
    sums = tie([sums], summed)[0]
    all_sums = mirror_gather(sum_over(sums, ("ctx", "tp")))
    total = tree_sum(all_sums)

    projector_sums = [
        lax.psum_scatter(half, "shard", scatter_dimension=0, tiled=True)
        for half in (early_projector, projector_half(head_rows[-1:]))
    ]
    grad_projector = jnp.concatenate(tie(projector_sums, *all_sums[1:]), 1)
    grad_projector = (
        grad_projector.astype(WIDE)
        .reshape(-1, heads, 3, HEAD_DIM)
        .transpose(0, 2, 1, 3)
        .reshape(-1, 3, local_width)
    )

    hidden_bias = lax.dynamic_index_in_dim(total[8:-2], lax.axis_index("tp"), 0, keepdims=False)
    projector_bias_sums = lax.dynamic_slice_in_dim(
        total[-2:], lax.axis_index("tp") * local_width, local_width, 1
    )
    total_settings = total[:6].reshape(-1)
    all_settings = jnp.concatenate([part[:6] for part in all_sums], 0).reshape(shard_size, -1)
    gate_terms = lax.dot_general(
        all_settings, modulator.astype(WIDE), (((1,), (1,)), ((), ())), precision=PRECISE
    )
    gate_terms = in_shard_order(mirror_exchange([gate_terms[r : r + 1] for r in range(shard_size)]))
    _, silu_back = jax.vjp(silu_gate, condition.astype(WIDE))
    grad_condition = silu_back(jnp.concatenate(gate_terms, 1))[0]
    column_count = all_settings.shape[1] // tp_size
    tp_settings = lax.dynamic_slice_in_dim(
        all_settings, lax.axis_index("tp") * column_count, column_count, 1
    )
    tp_scaled = lax.dynamic_slice_in_dim(
        scaled_all.astype(WIDE), place + core * row_count, row_count, 1
    )
    grad_modulator = lax.dot_general(
        tp_scaled, tp_settings, (((0,), (0,)), ((), ())), precision=PRECISE
    )
    grad_modulator_bias = lax.dynamic_slice_in_dim(
        total_settings, lax.axis_index("tp") * column_count, column_count, 0
    )
    return (
        block_output[None],
        grad_latent[None],
        grad_condition,
        grad_modulator,
        grad_modulator_bias,
        grad_projector,
        projector_bias_sums,
        grad_merger,
        total[7],
        grad_expander,
        hidden_bias,
        grad_reducer,
        total[6],
    )


def solution(mesh):
    in_specs = (
        P("shard", ("ctx", "tp"), None),
        P("shard", None),
        P("shard", None),
        P(),
        P("shard", None, "tp"),
        P(None, "tp"),
        P("tp", "shard"),
        P(),
        P("shard", "tp"),
        P("tp"),
        P("tp", "shard"),
        P(),
        P("shard", ("ctx", "tp"), None),
    )
    out_specs = (
        P("shard", ("ctx", "tp"), None),
        P("shard", ("ctx", "tp"), None),
        P("shard", None),
        P(("shard", "ctx"), "tp"),
        P("tp"),
        P(("shard", "ctx"), None, "tp"),
        P(None, "tp"),
        P("tp", ("shard", "ctx")),
        P(),
        P(("shard", "ctx"), "tp"),
        P("tp"),
        P("tp", ("shard", "ctx")),
        P(),
    )
    return jax.shard_map(shards, mesh=mesh, in_specs=in_specs, out_specs=out_specs, check_vma=False)
```

```python
import functools
import math

import jax
import jax.numpy as jnp
from jax import lax
from jax.experimental import pallas as pl
from jax.experimental.pallas import tpu as pltpu
from jax.sharding import PartitionSpec as P

HEAD_DIM = 64
PRECISE = lax.Precision.HIGHEST
LOW = jnp.bfloat16
WIDE = jnp.float32


def layer_norm(values):
    row_mean = jnp.mean(values, -1, keepdims=True)
    centered = values - row_mean
    variance = jnp.mean(centered * centered, -1, keepdims=True)
    return centered * lax.rsqrt(variance + 1e-06)


def gelu_tanh(values):
    return (
        0.5
        * values
        * (1.0 + jnp.tanh(0.7978845608028654 * (values + 0.044715 * values * values * values)))
    )


def silu_gate(values):
    return values * jax.nn.sigmoid(values)


def modulate(values, scale_part, shift_part):
    return layer_norm(values) * (1.0 + scale_part) + shift_part


def dot_wide(left, right, left_dim, right_dim):
    return lax.dot_general(
        left, right, (((left_dim,), (right_dim,)), ((), ())), preferred_element_type=WIDE
    )


def gather_list(block, axis):
    count = lax.axis_size(axis)
    return [block] + [
        lax.ppermute(block, axis, [(i, (i - r) % count) for i in range(count)])
        for r in range(1, count)
    ]


def scatter_list(blocks, axis):
    count = lax.axis_size(axis)
    arrived = {
        (count - r) % count: lax.ppermute(
            blocks[r], axis, [(i, (i + r) % count) for i in range(count)]
        )
        for r in range(1, count)
    }
    arrived[0] = blocks[0]
    return [arrived[r] for r in range(count)]


def swap_ctx(block):
    count = lax.axis_size("ctx")
    return lax.ppermute(block, "ctx", [(i, (i + 1) % count) for i in range(count)])


def sum_over(value, axes):
    for axis in axes:
        step = 1
        while step < lax.axis_size(axis):
            value = value + lax.ppermute(
                value, axis, [(i, i ^ step) for i in range(lax.axis_size(axis))]
            )
            step *= 2
    return value


def rotated(rows, start):
    return lax.dynamic_slice_in_dim(jnp.concatenate([rows, rows], 0), start, rows.shape[0], 0)


def mirror(block, r):
    return lax.ppermute(block, "shard", [(i, i ^ r) for i in range(lax.axis_size("shard"))])


def mirror_gather(block):
    return [block] + [mirror(block, r) for r in range(1, lax.axis_size("shard"))]


def mirror_exchange(blocks):
    return [blocks[0]] + [mirror(block, r) for r, block in enumerate(blocks) if r > 0]


def in_shard_order(blocks):
    own, bit = lax.axis_index("shard"), 1
    while bit < len(blocks):
        flip = (own & bit) != 0
        blocks = [jnp.where(flip, blocks[j ^ bit], blocks[j]) for j in range(len(blocks))]
        bit *= 2
    return blocks


def tree_sum(blocks):
    while len(blocks) > 1:
        blocks = [blocks[i] + blocks[i + 1] for i in range(0, len(blocks), 2)]
    return blocks[0]


def ordered_call(kernel, operands, in_specs, out_specs, out_shape, before=(), through=(), **rest):
    count, through_count, results = len(operands), len(through), len(out_specs)
    extra = through_count + len(before)
    unread = pl.BlockSpec(memory_space=pl.ANY)

    def body(*refs):
        after_inputs = refs[count + extra :]
        kernel(*refs[:count], *after_inputs[:results], *after_inputs[results + through_count :])

    made = pl.pallas_call(
        body,
        in_specs=list(in_specs) + [unread] * extra,
        out_specs=list(out_specs) + [unread] * through_count,
        out_shape=list(out_shape) + [jax.ShapeDtypeStruct(x.shape, x.dtype) for x in through],
        input_output_aliases={count + i: results + i for i in range(through_count)},
        **rest,
    )(*operands, *through, *before)
    return made[:results], made[results:]


def tie(values, *before):
    return ordered_call(
        lambda *refs: None,
        (),
        (),
        (),
        (),
        before,
        values,
        cost_estimate=pl.CostEstimate(flops=1, bytes_accessed=1, transcendentals=0),
    )[1]


def attend_kernel(query_ref, key_ref, value_ref, far_key_ref, far_value_ref, out_ref, stat_ref, key_rows):
    near = key_ref.shape[2]
    key_rows[:near, :] = key_ref[0].T
    key_rows[near:, :] = far_key_ref[0].T
    queries = query_ref[0] * jnp.array(HEAD_DIM ** (-0.5), LOW)
    columns = queries.shape[1]
    top = total = mixed = None
    for half, values in enumerate((value_ref, far_value_ref)):
        scores = jnp.dot(
            key_rows[half * near : (half + 1) * near, :], queries, preferred_element_type=WIDE
        )
        block_top = jnp.max(scores, 0, keepdims=True)
        new_top = block_top if top is None else jnp.maximum(top, block_top)
        exponent = jnp.exp(scores - new_top)
        block_total = jnp.sum(exponent, 0, keepdims=True)
        block_mixed = jnp.dot(values[0], exponent.astype(LOW), preferred_element_type=WIDE)
        if top is None:
            total, mixed = block_total, block_mixed
        else:
            fade = jnp.exp(top - new_top)
            total = total * fade + block_total
            mixed = mixed * fade + block_mixed
        top = new_top
    out_ref[0] = (mixed / total).astype(LOW)
    stat_ref[0] = top + jnp.log(total)


def attend(near_rows, far_rows, place, width, before=(), through=()):
    heads, _, tokens = near_rows.shape
    size = HEAD_DIM

    def whole(row):
        return pl.BlockSpec((1, size, tokens), lambda h: (h, row, 0))

    return ordered_call(
        attend_kernel,
        (near_rows, near_rows, near_rows, far_rows, far_rows),
        grid=(heads,),
        in_specs=[
            pl.BlockSpec((1, size, width), lambda h: (h, 0, place)),
            whole(1),
            whole(2),
            whole(0),
            whole(1),
        ],
        out_specs=[
            pl.BlockSpec((1, size, width), lambda h: (h, 0, 0)),
            pl.BlockSpec((1, 1, width), lambda h: (h, 0, 0)),
        ],
        out_shape=[
            jax.ShapeDtypeStruct((heads, size, width), LOW),
            jax.ShapeDtypeStruct((heads, 1, width), WIDE),
        ],
        scratch_shapes=[pltpu.VMEM((2 * tokens, size), LOW)],
        compiler_params=pltpu.CompilerParams(vmem_limit_bytes=48 * 2**20),
        cost_estimate=pl.CostEstimate(
            flops=heads * 2 * tokens * width * size * 4 * 4,
            bytes_accessed=heads * size * (width * 4 + tokens * 8),
            transcendentals=heads * 2 * tokens * width,
        ),
        before=before,
        through=through,
    )


def with_parts(rows, extra):
    high = extra.astype(LOW)
    rest = extra - high.astype(WIDE)
    middle = rest.astype(LOW)
    lowest = (rest - middle.astype(WIDE)).astype(LOW)
    fill = jnp.zeros((HEAD_DIM - 3, rows.shape[1]), LOW)
    return jnp.concatenate([rows, high, middle, lowest, fill], 0)


def attend_back_kernel(
    key_block, query_block, first,
    query_ref, key_ref, value_ref, grad_ref, out_ref, stat_ref, sum_ref,
    grad_query_ref, grad_pair_ref,
    key_rows, value_rows, query_rows, grad_rows, query_more, grad_more, query_sum,
):
    size = HEAD_DIM
    tokens = query_ref.shape[2]
    keys_held = key_ref.shape[2]
    queries = query_ref[0] * jnp.array(size ** (-0.5), LOW)
    grads = grad_ref[0]
    ones = jnp.where(lax.broadcasted_iota(jnp.int32, (keys_held, size), 1) < 3, 1.0, 0.0).astype(LOW)
    key_rows[:, :size] = key_ref[0].T
    key_rows[:, size:] = ones
    value_rows[:, :size] = value_ref[0].T
    value_rows[:, size:] = ones
    query_rows[...] = queries.T
    grad_rows[...] = grads.T
    inner = jnp.sum(grads.astype(WIDE) * out_ref[0].astype(WIDE), 0, keepdims=True)
    query_more[...] = with_parts(queries, -stat_ref[0])
    grad_more[...] = with_parts(grads, -inner)
    query_sum[...] = jnp.zeros_like(query_sum) if first else sum_ref[0]

    def step(index, carry):
        place = pl.ds(pl.multiple_of(index * key_block, key_block), key_block)
        keys, values, columns = key_rows[place, :], value_rows[place, :], key_ref[0, :, place]
        key_sum = jnp.zeros((key_block, size), WIDE)
        value_sum = jnp.zeros((key_block, size), WIDE)
        for part in range(tokens // query_block):
            span = slice(part * query_block, (part + 1) * query_block)
            probs = jnp.exp(jnp.dot(keys, query_more[:, span], preferred_element_type=WIDE))
            centered = jnp.dot(values, grad_more[:, span], preferred_element_type=WIDE)
            grad_scores = (probs * centered).astype(LOW)
            value_sum += jnp.dot(probs.astype(LOW), grad_rows[span, :], preferred_element_type=WIDE)
            key_sum += jnp.dot(grad_scores, query_rows[span, :], preferred_element_type=WIDE)
            query_sum[:, span] += jnp.dot(columns, grad_scores, preferred_element_type=WIDE)
        grad_pair_ref[0, :size, place] = key_sum.T.astype(LOW)
        grad_pair_ref[0, size:, place] = value_sum.T.astype(LOW)
        return carry

    lax.fori_loop(0, keys_held // key_block, step, 0)
    if first:
        grad_query_ref[0] = query_sum[...]
    else:
        grad_query_ref[0] = (query_sum[...] * size ** (-0.5)).astype(LOW)


def attend_back(head, near_rows, pair_rows, key_place, grads, outs, stats, query_sum, before=(), through=()):
    tokens = near_rows.shape[2]
    size = HEAD_DIM
    key_block, query_block = math.gcd(tokens, 1024), math.gcd(tokens, 512)
    first = query_sum is None
    if first:
        query_sum = jnp.zeros((1, 8, 128), WIDE)

    def rows(count, place=0):
        return pl.BlockSpec((1, count, tokens), lambda i: (head, place, 0))

    def result(count):
        return pl.BlockSpec((1, count, tokens), lambda i: (0, 0, 0))

    return ordered_call(
        functools.partial(attend_back_kernel, key_block, query_block, first),
        (near_rows, pair_rows, pair_rows, grads, outs, stats, query_sum),
        grid=(1,),
        in_specs=[
            rows(size),
            rows(size, key_place),
            rows(size, key_place + 1),
            rows(size),
            rows(size),
            rows(1),
            pl.BlockSpec(query_sum.shape, lambda i: (0, 0, 0)),
        ],
        out_specs=[result(size), result(2 * size)],
        out_shape=[
            jax.ShapeDtypeStruct((1, size, tokens), WIDE if first else LOW),
            jax.ShapeDtypeStruct((1, 2 * size, tokens), LOW),
        ],
        scratch_shapes=[
            pltpu.VMEM((tokens, 2 * size), LOW),
            pltpu.VMEM((tokens, 2 * size), LOW),
            pltpu.VMEM((tokens, size), LOW),
            pltpu.VMEM((tokens, size), LOW),
            pltpu.VMEM((2 * size, tokens), LOW),
            pltpu.VMEM((2 * size, tokens), LOW),
            pltpu.VMEM((size, tokens), WIDE),
        ],
        compiler_params=pltpu.CompilerParams(vmem_limit_bytes=48 * 2**20),
        cost_estimate=pl.CostEstimate(
            flops=tokens * tokens * size * 10 * 4,
            bytes_accessed=size * tokens * 2 * 9,
            transcendentals=tokens * tokens,
        ),
        before=before,
        through=through,
    )


def weight_kernel(
    normed_ref, hidden_ref, far_hidden_ref, feed_ref, active_ref, far_active_ref, branch_ref, heads_ref,
    near_ref, far_ref,
    normed_columns, feed_columns, branch_columns,
):
    @pl.when(pl.program_id(0) == 0)
    def _():
        normed_columns[...] = normed_ref[...].T
        feed_columns[...] = feed_ref[...].T
        branch_columns[...] = branch_ref[...].T

    units, features = hidden_ref.shape[1], heads_ref.shape[0]
    merger = dot_wide(branch_columns[...], heads_ref[...], 1, 1).astype(LOW)
    for made_ref, hidden, active in (
        (near_ref, hidden_ref, active_ref),
        (far_ref, far_hidden_ref, far_active_ref),
    ):
        for start, left, right in ((0, normed_columns, hidden), (units, feed_columns, active)):
            made_ref[:, start : start + units] = jnp.dot(
                left[...], right[...], preferred_element_type=WIDE
            ).astype(LOW)
        made_ref[:, 2 * units :] = jnp.zeros((made_ref.shape[0], made_ref.shape[1] - 2 * units), LOW)
        made_ref[:, 2 * units : 2 * units + features] = merger


def padded_columns(count):
    return -(-count // 128) * 128


def weight_terms(normed, grad_hidden, grad_feed, activated, grad_branch, attended, steps):
    tokens, width = normed.shape
    units, features = grad_hidden[0].shape[1] // steps, attended.shape[0] // steps
    columns = padded_columns(2 * units + features)

    def whole(array):
        return pl.BlockSpec(array.shape, lambda i: (0, 0))

    taken = pl.BlockSpec((tokens, units), lambda i: (0, i))
    made = pl.BlockSpec((width, columns), lambda i: (0, i))
    return pl.pallas_call(
        weight_kernel,
        grid=(steps,),
        in_specs=[whole(normed), taken, taken, whole(grad_feed), taken, taken]
        + [whole(grad_branch), pl.BlockSpec((features, tokens), lambda i: (i, 0))],
        out_specs=[made] * 2,
        out_shape=[jax.ShapeDtypeStruct((width, steps * columns), LOW)] * 2,
        scratch_shapes=[pltpu.VMEM((width, tokens), LOW)] * 3,
        compiler_params=pltpu.CompilerParams(vmem_limit_bytes=48 * 2**20),
        cost_estimate=pl.CostEstimate(
            flops=2 * tokens * width * steps * (4 * units + features),
            bytes_accessed=2**25,
            transcendentals=0,
        ),
    )(normed, *grad_hidden, grad_feed, *activated, grad_branch, attended)


def core_half(grad):
    ctx_size, shard_size = lax.axis_size("ctx"), lax.axis_size("shard")
    rows = grad.shape[0] // (shard_size * ctx_size)
    low = grad.astype(LOW).reshape(shard_size, ctx_size, rows, grad.shape[1])
    core = lax.axis_index("ctx")
    mine = lax.dynamic_index_in_dim(low, core, 1, keepdims=False)
    theirs = lax.dynamic_index_in_dim(low, 1 - core, 1, keepdims=False)
    return (
        mine.reshape(shard_size * rows, grad.shape[1]),
        theirs.reshape(shard_size * rows, grad.shape[1]),
    )


def sum_low(left, right):
    return (left.astype(WIDE) + right.astype(WIDE)).astype(LOW)


def shards(
    latent,
    condition,
    modulator,
    modulator_bias,
    projector,
    projector_bias,
    merger,
    merger_bias,
    expander,
    expander_bias,
    reducer,
    reducer_bias,
    cotangent,
):
    tp_size, ctx_size, shard_size = (lax.axis_size(axis) for axis in ("tp", "ctx", "shard"))
    core = lax.axis_index("ctx")
    own_latent, own_cotangent = latent[0], cotangent[0]
    block, model_width = own_latent.shape
    local_width = projector.shape[2]
    heads = local_width // HEAD_DIM
    head_columns = 3 * HEAD_DIM
    local_hidden = expander.shape[1]
    half_hidden = local_hidden // ctx_size
    kept_rows = projector.shape[0]
    place = lax.axis_index("shard") * kept_rows

    conditions = jnp.concatenate(mirror_gather(condition.astype(WIDE)), 0)
    def half_units(weight, axis):
        return lax.dynamic_slice_in_dim(weight, core * half_hidden, half_hidden, axis)

    share = tp_size * half_hidden
    latent_blocks = gather_list(own_latent, "tp")
    own_reducer = lax.all_gather(
        jnp.concatenate(gather_list(half_units(reducer, 0).T, "tp"), 1), "shard", axis=0, tiled=True
    )

    scaled_all = silu_gate(conditions).astype(LOW)
    terms = jnp.dot(
        lax.dynamic_slice_in_dim(scaled_all, place, kept_rows, 1),
        modulator,
        preferred_element_type=WIDE,
    )
    terms = mirror_exchange([terms[r : r + 1] for r in range(shard_size)])
    modulation = tree_sum(terms) + modulator_bias.astype(WIDE)

    own_projector = (
        projector.reshape(kept_rows, 3, heads, HEAD_DIM)
        .transpose(0, 2, 1, 3)
        .reshape(kept_rows, 3 * local_width)
    )
    head_projector = jnp.concatenate(in_shard_order(mirror_gather(own_projector)), 0)
    zero_bias = jnp.zeros((1, local_width), projector_bias.dtype)
    qkv_bias = (
        jnp.concatenate([projector_bias[:1], zero_bias, projector_bias[1:]], 0)
        .reshape(3, heads, HEAD_DIM)
        .transpose(1, 0, 2)
        .reshape(3 * local_width, 1)
        .astype(WIDE)
    )
    settings = [
        modulation[:, index * model_width : (index + 1) * model_width] for index in range(6)
    ]
    shift_one, scale_one, gate_one, shift_two, scale_two, gate_two = settings

    latent_blocks = [latent_blocks[0], *tie(latent_blocks[1:], head_projector, modulation)]
    normed_rows = jnp.concatenate(
        [modulate(rows.astype(WIDE), scale_one, shift_one).astype(LOW) for rows in latent_blocks], 0
    )
    tokens = normed_rows.shape[0]
    projected = (dot_wide(head_projector, normed_rows, 0, 1) + qkv_bias).astype(LOW)
    near_rows = projected.reshape(heads, head_columns, tokens)
    far_rows = swap_ctx(near_rows[:, HEAD_DIM:, :])

    bias_rows = jnp.zeros((16, half_hidden + local_width), expander_bias.dtype)
    for index, part in enumerate((core, 1 - core)):
        half_bias = lax.dynamic_slice_in_dim(expander_bias, part * half_hidden, half_hidden, 0)
        bias_rows = bias_rows.at[index, :half_hidden].set(half_bias)
    pieces = jnp.concatenate([half_units(expander, 1), merger.T], 1)
    pieces = jnp.concatenate([pieces, bias_rows], 0)
    pieces = gather_list(tie([pieces], *latent_blocks[1:])[0], "tp")
    pieces = tie(pieces, near_rows)
    own_expander = lax.all_gather(
        jnp.concatenate([piece[:kept_rows, :half_hidden] for piece in pieces], 1),
        "shard",
        axis=0,
        tiled=True,
    )
    full_merger = lax.all_gather(
        jnp.concatenate([piece[:kept_rows, half_hidden:] for piece in pieces], 1),
        "shard",
        axis=0,
        tiled=True,
    )
    part_biases = [
        jnp.concatenate(
            [piece[kept_rows + index : kept_rows + index + 1, :half_hidden] for piece in pieces], 1
        )
        for index in range(2)
    ]
    outs, stats, sent = [None] * tp_size, [None] * tp_size, [None] * tp_size
    order = sorted(range(tp_size), key=lambda r: -min(r, tp_size - r))
    previous = ()
    for r in order:
        (outs[r], stats[r]), _ = attend(near_rows, far_rows, r, block, previous)
        sent[r] = outs[r].reshape(local_width, block)
        previous = (outs[r],)
    attended = jnp.concatenate(scatter_list(sent, "tp"), 0)
    all_outs, all_stats = jnp.concatenate(outs, 2), jnp.concatenate(stats, 2)

    own_expander, full_merger = tie([own_expander, full_merger], outs[order[-1]])
    expanders = [own_expander, swap_ctx(own_expander)]
    reducers = [own_reducer, swap_ctx(own_reducer)]
    core_width = model_width // ctx_size
    tail_projector = lax.dynamic_slice_in_dim(head_projector, core * core_width, core_width, 0).T
    projectors = lax.all_gather(
        tie([tail_projector], outs[order[-1]])[0], "tp", axis=0, tiled=True
    )
    latent_wide = own_latent.astype(WIDE)
    branch = dot_wide(attended, full_merger, 0, 1) + merger_bias.astype(WIDE)
    middle = latent_wide + gate_one * branch
    normed_two_wide, norm_back_two = jax.vjp(modulate, middle, scale_two, shift_two)
    normed_two = normed_two_wide.astype(LOW)
    grad_output = own_cotangent.astype(WIDE)
    grad_feed = (gate_two * grad_output).astype(LOW)
    feed, grad_normed_two = reducer_bias.astype(WIDE), 0.0
    activated, grad_hidden = [], []
    for full_expander, full_reducer, part_bias in zip(expanders, reducers, part_biases):
        hidden = dot_wide(normed_two, full_expander, 1, 0) + part_bias.astype(WIDE)
        active, gelu_back = jax.vjp(gelu_tanh, hidden)
        activated.append(active.astype(LOW))
        feed = feed + dot_wide(activated[-1], full_reducer, 1, 1)
        grad_hidden.append(gelu_back(dot_wide(grad_feed, full_reducer, 1, 0))[0].astype(LOW))
        grad_normed_two = grad_normed_two + dot_wide(grad_hidden[-1], full_expander, 1, 1)
    block_output = (middle + gate_two * feed).astype(LOW)
    grad_gate_two = jnp.sum(grad_output * feed, 0, keepdims=True)
    grad_middle_norm, grad_scale_two, grad_shift_two = norm_back_two(grad_normed_two)
    grad_middle = grad_output + grad_middle_norm
    grad_gate_one = jnp.sum(grad_middle * branch, 0, keepdims=True)
    grad_branch = (gate_one * grad_middle).astype(LOW)
    grad_attended = dot_wide(full_merger, grad_branch, 0, 1).astype(LOW)
    grad_blocks = scatter_list(
        [grad_attended[r * local_width : (r + 1) * local_width] for r in range(tp_size)], "tp"
    )

    weight_near, weight_far = weight_terms(
        normed_two, grad_hidden, grad_feed, activated, grad_branch, attended, tp_size
    )
    all_grads = jnp.concatenate(grad_blocks, 1).reshape(heads, HEAD_DIM, tokens)

    def in_order(left, right, axis):
        return jnp.where(
            core == 0, jnp.concatenate([left, right], axis), jnp.concatenate([right, left], axis)
        )

    tp_turn = lax.rem(tp_size - lax.axis_index("tp"), tp_size)
    hidden_sums = in_order(
        *(jnp.sum(part, 0, dtype=WIDE).reshape(tp_size, half_hidden) for part in grad_hidden), 1
    )
    early_sums = jnp.concatenate(
        [
            grad_gate_one,
            grad_shift_two,
            grad_scale_two,
            grad_gate_two,
            jnp.sum(grad_feed, 0, keepdims=True, dtype=WIDE),
            jnp.sum(grad_branch, 0, keepdims=True, dtype=WIDE),
            rotated(hidden_sums, tp_turn),
        ],
        0,
    )

    def projector_half(rows):
        own, other = core_half(dot_wide(normed_rows, jnp.concatenate(rows, 0), 0, 1))
        return sum_low(own, swap_ctx(other))

    head_rows, arrived_rows = [], []
    for head in range(heads):
        before = ()
        if head == 1:
            before = (head_rows[0],)
        elif head == 2:
            before = (head_rows[1], *arrived_rows[0])
        (partial, far), _ = attend_back(
            head, near_rows, far_rows, 0, all_grads, all_outs, all_stats, None, before
        )
        before = ()
        if head == 0:
            (weight_came,) = tie([swap_ctx(weight_far)], partial)
            weight_half = sum_low(weight_near, weight_came)
            weight_sum = lax.psum_scatter(weight_half, "shard", scatter_dimension=0, tiled=True)
            before = (weight_half,)
        elif head == 1:
            projectors = tie([projectors], partial)[0]
            other_projectors = swap_ctx(projectors)
        elif head == 2:
            early_projector = projector_half(head_rows)
            before = (other_projectors, *arrived_rows[1], early_projector)
        far_came = swap_ctx(far[0])
        (grad_query, near), _ = attend_back(
            head, near_rows, near_rows, 1, all_grads, all_outs, all_stats, partial, before
        )
        rows = jnp.concatenate([grad_query[0], sum_low(near[0], far_came)], 0)
        head_rows.append(rows)
        arrived_rows.append(
            scatter_list([rows[:, r * block : (r + 1) * block] for r in range(tp_size)], "tp")
        )
    rows = jnp.zeros((tp_size * heads * head_columns, block), LOW)
    for head, arrived in enumerate(arrived_rows):
        for r, part in enumerate(arrived):
            turn = lax.rem(lax.axis_index("tp") + r, tp_size)
            rows = lax.dynamic_update_slice_in_dim(
                rows, part, (turn * heads + head) * head_columns, 0
            )
    grad_normed = in_order(
        *(dot_wide(rows, part, 0, 0) for part in (projectors, other_projectors)), 1
    )
    _, norm_back = jax.vjp(modulate, latent_wide, scale_one, shift_one)
    grad_latent_norm, grad_scale_one, grad_shift_one = norm_back(grad_normed)
    grad_latent = grad_middle + grad_latent_norm

    def from_peers(columns):
        width = columns.shape[1] // tp_size
        parts = scatter_list([columns[:, r * width : (r + 1) * width] for r in range(tp_size)], "tp")
        return sum(part.astype(WIDE) for part in parts)

    row_count = kept_rows // ctx_size
    summed = from_peers(weight_sum)
    two = summed[:, : 2 * half_hidden]
    own_two = lax.dynamic_slice_in_dim(two, core * row_count, row_count, 0)
    other_two = swap_ctx(lax.dynamic_slice_in_dim(two, (1 - core) * row_count, row_count, 0))
    grad_expander = in_order(own_two[:, :half_hidden], other_two[:, :half_hidden], 1)
    grad_reducer = in_order(own_two[:, half_hidden:], other_two[:, half_hidden:], 1).T
    grad_merger = lax.dynamic_slice_in_dim(summed[:, 2 * half_hidden : 2 * half_hidden + local_width], core * row_count, row_count, 0).T

    column_sums = jnp.sum(jnp.concatenate(head_rows, 0), 1, dtype=WIDE).reshape(heads, 3, HEAD_DIM)
    bias_sums = jnp.stack([column_sums[:, 0].reshape(-1), column_sums[:, 2].reshape(-1)])
    bias_sums = lax.dynamic_update_slice_in_dim(
        jnp.zeros((2, model_width), WIDE), bias_sums, lax.axis_index("tp") * local_width, 1
    )
    sums = jnp.concatenate([grad_shift_one, grad_scale_one, early_sums, bias_sums], 0)
    sums = tie([sums], summed)[0]
    all_sums = mirror_gather(sum_over(sums, ("ctx", "tp")))
    total = tree_sum(all_sums)

    projector_sums = [
        lax.psum_scatter(half, "shard", scatter_dimension=0, tiled=True)
        for half in (early_projector, projector_half(head_rows[-1:]))
    ]
    grad_projector = jnp.concatenate(tie(projector_sums, *all_sums[1:]), 1)
    grad_projector = (
        grad_projector.astype(WIDE)
        .reshape(-1, heads, 3, HEAD_DIM)
        .transpose(0, 2, 1, 3)
        .reshape(-1, 3, local_width)
    )

    hidden_bias = lax.dynamic_index_in_dim(total[8:-2], lax.axis_index("tp"), 0, keepdims=False)
    projector_bias_sums = lax.dynamic_slice_in_dim(
        total[-2:], lax.axis_index("tp") * local_width, local_width, 1
    )
    total_settings = total[:6].reshape(-1)
    all_settings = jnp.concatenate([part[:6] for part in all_sums], 0).reshape(shard_size, -1)
    gate_terms = lax.dot_general(
        all_settings, modulator.astype(WIDE), (((1,), (1,)), ((), ())), precision=PRECISE
    )
    gate_terms = in_shard_order(mirror_exchange([gate_terms[r : r + 1] for r in range(shard_size)]))
    _, silu_back = jax.vjp(silu_gate, condition.astype(WIDE))
    grad_condition = silu_back(jnp.concatenate(gate_terms, 1))[0]
    column_count = all_settings.shape[1] // tp_size
    tp_settings = lax.dynamic_slice_in_dim(
        all_settings, lax.axis_index("tp") * column_count, column_count, 1
    )
    tp_scaled = lax.dynamic_slice_in_dim(
        scaled_all.astype(WIDE), place + core * row_count, row_count, 1
    )
    grad_modulator = lax.dot_general(
        tp_scaled, tp_settings, (((0,), (0,)), ((), ())), precision=PRECISE
    )
    grad_modulator_bias = lax.dynamic_slice_in_dim(
        total_settings, lax.axis_index("tp") * column_count, column_count, 0
    )
    return (
        block_output[None],
        grad_latent[None],
        grad_condition,
        grad_modulator,
        grad_modulator_bias,
        grad_projector,
        projector_bias_sums,
        grad_merger,
        total[7],
        grad_expander,
        hidden_bias,
        grad_reducer,
        total[6],
    )


def solution(mesh):
    in_specs = (
        P("shard", ("ctx", "tp"), None),
        P("shard", None),
        P("shard", None),
        P(),
        P("shard", None, "tp"),
        P(None, "tp"),
        P("tp", "shard"),
        P(),
        P("shard", "tp"),
        P("tp"),
        P("tp", "shard"),
        P(),
        P("shard", ("ctx", "tp"), None),
    )
    out_specs = (
        P("shard", ("ctx", "tp"), None),
        P("shard", ("ctx", "tp"), None),
        P("shard", None),
        P(("shard", "ctx"), "tp"),
        P("tp"),
        P(("shard", "ctx"), None, "tp"),
        P(None, "tp"),
        P("tp", ("shard", "ctx")),
        P(),
        P(("shard", "ctx"), "tp"),
        P("tp"),
        P("tp", ("shard", "ctx")),
        P(),
    )
    return jax.shard_map(shards, mesh=mesh, in_specs=in_specs, out_specs=out_specs, check_vma=False)
```

```python
import functools
import math

import jax
import jax.numpy as jnp
from jax import lax
from jax.experimental import pallas as pl
from jax.experimental.pallas import tpu as pltpu
from jax.sharding import PartitionSpec as P

HEAD_DIM = 64
PRECISE = lax.Precision.HIGHEST
LOW = jnp.bfloat16
WIDE = jnp.float32


def layer_norm(values):
    row_mean = jnp.mean(values, -1, keepdims=True)
    centered = values - row_mean
    variance = jnp.mean(centered * centered, -1, keepdims=True)
    return centered * lax.rsqrt(variance + 1e-06)


def gelu_tanh(values):
    return (
        0.5
        * values
        * (1.0 + jnp.tanh(0.7978845608028654 * (values + 0.044715 * values * values * values)))
    )


def silu_gate(values):
    return values * jax.nn.sigmoid(values)


def modulate(values, scale_part, shift_part):
    return layer_norm(values) * (1.0 + scale_part) + shift_part


def dot_wide(left, right, left_dim, right_dim):
    return lax.dot_general(
        left, right, (((left_dim,), (right_dim,)), ((), ())), preferred_element_type=WIDE
    )


def gather_list(block, axis):
    count = lax.axis_size(axis)
    return [block] + [
        lax.ppermute(block, axis, [(i, (i - r) % count) for i in range(count)])
        for r in range(1, count)
    ]


def scatter_list(blocks, axis):
    count = lax.axis_size(axis)
    arrived = {
        (count - r) % count: lax.ppermute(
            blocks[r], axis, [(i, (i + r) % count) for i in range(count)]
        )
        for r in range(1, count)
    }
    arrived[0] = blocks[0]
    return [arrived[r] for r in range(count)]


def swap_ctx(block):
    count = lax.axis_size("ctx")
    return lax.ppermute(block, "ctx", [(i, (i + 1) % count) for i in range(count)])


def sum_over(value, axes):
    for axis in axes:
        step = 1
        while step < lax.axis_size(axis):
            value = value + lax.ppermute(
                value, axis, [(i, i ^ step) for i in range(lax.axis_size(axis))]
            )
            step *= 2
    return value


def rotated(rows, start):
    return lax.dynamic_slice_in_dim(jnp.concatenate([rows, rows], 0), start, rows.shape[0], 0)


def mirror(block, r):
    return lax.ppermute(block, "shard", [(i, i ^ r) for i in range(lax.axis_size("shard"))])


def mirror_gather(block):
    return [block] + [mirror(block, r) for r in range(1, lax.axis_size("shard"))]


def mirror_exchange(blocks):
    return [blocks[0]] + [mirror(block, r) for r, block in enumerate(blocks) if r > 0]


def in_shard_order(blocks):
    own, bit = lax.axis_index("shard"), 1
    while bit < len(blocks):
        flip = (own & bit) != 0
        blocks = [jnp.where(flip, blocks[j ^ bit], blocks[j]) for j in range(len(blocks))]
        bit *= 2
    return blocks


def tree_sum(blocks):
    while len(blocks) > 1:
        blocks = [blocks[i] + blocks[i + 1] for i in range(0, len(blocks), 2)]
    return blocks[0]


def ordered_call(kernel, operands, in_specs, out_specs, out_shape, before=(), through=(), **rest):
    count, through_count, results = len(operands), len(through), len(out_specs)
    extra = through_count + len(before)
    unread = pl.BlockSpec(memory_space=pl.ANY)

    def body(*refs):
        after_inputs = refs[count + extra :]
        kernel(*refs[:count], *after_inputs[:results], *after_inputs[results + through_count :])

    made = pl.pallas_call(
        body,
        in_specs=list(in_specs) + [unread] * extra,
        out_specs=list(out_specs) + [unread] * through_count,
        out_shape=list(out_shape) + [jax.ShapeDtypeStruct(x.shape, x.dtype) for x in through],
        input_output_aliases={count + i: results + i for i in range(through_count)},
        **rest,
    )(*operands, *through, *before)
    return made[:results], made[results:]


def tie(values, *before):
    return ordered_call(
        lambda *refs: None,
        (),
        (),
        (),
        (),
        before,
        values,
        cost_estimate=pl.CostEstimate(flops=1, bytes_accessed=1, transcendentals=0),
    )[1]


def attend_kernel(query_ref, key_ref, value_ref, far_key_ref, far_value_ref, out_ref, stat_ref, key_rows):
    near = key_ref.shape[2]
    key_rows[:near, :] = key_ref[0].T
    key_rows[near:, :] = far_key_ref[0].T
    queries = query_ref[0] * jnp.array(HEAD_DIM ** (-0.5), LOW)
    columns = queries.shape[1]
    top = total = mixed = None
    for half, values in enumerate((value_ref, far_value_ref)):
        scores = jnp.dot(
            key_rows[half * near : (half + 1) * near, :], queries, preferred_element_type=WIDE
        )
        block_top = jnp.max(scores, 0, keepdims=True)
        new_top = block_top if top is None else jnp.maximum(top, block_top)
        exponent = jnp.exp(scores - new_top)
        block_total = jnp.sum(exponent, 0, keepdims=True)
        block_mixed = jnp.dot(values[0], exponent.astype(LOW), preferred_element_type=WIDE)
        if top is None:
            total, mixed = block_total, block_mixed
        else:
            fade = jnp.exp(top - new_top)
            total = total * fade + block_total
            mixed = mixed * fade + block_mixed
        top = new_top
    out_ref[0] = (mixed / total).astype(LOW)
    stat_ref[0] = top + jnp.log(total)


def attend(near_rows, far_rows, place, width, before=(), through=()):
    heads, _, tokens = near_rows.shape
    size = HEAD_DIM

    def whole(row):
        return pl.BlockSpec((1, size, tokens), lambda h: (h, row, 0))

    return ordered_call(
        attend_kernel,
        (near_rows, near_rows, near_rows, far_rows, far_rows),
        grid=(heads,),
        in_specs=[
            pl.BlockSpec((1, size, width), lambda h: (h, 0, place)),
            whole(1),
            whole(2),
            whole(0),
            whole(1),
        ],
        out_specs=[
            pl.BlockSpec((1, size, width), lambda h: (h, 0, 0)),
            pl.BlockSpec((1, 1, width), lambda h: (h, 0, 0)),
        ],
        out_shape=[
            jax.ShapeDtypeStruct((heads, size, width), LOW),
            jax.ShapeDtypeStruct((heads, 1, width), WIDE),
        ],
        scratch_shapes=[pltpu.VMEM((2 * tokens, size), LOW)],
        compiler_params=pltpu.CompilerParams(vmem_limit_bytes=48 * 2**20),
        cost_estimate=pl.CostEstimate(
            flops=heads * 2 * tokens * width * size * 4 * 4,
            bytes_accessed=heads * size * (width * 4 + tokens * 8),
            transcendentals=heads * 2 * tokens * width,
        ),
        before=before,
        through=through,
    )


def with_parts(rows, extra):
    high = extra.astype(LOW)
    rest = extra - high.astype(WIDE)
    middle = rest.astype(LOW)
    lowest = (rest - middle.astype(WIDE)).astype(LOW)
    fill = jnp.zeros((HEAD_DIM - 3, rows.shape[1]), LOW)
    return jnp.concatenate([rows, high, middle, lowest, fill], 0)


def attend_back_kernel(
    key_block, query_block, first,
    query_ref, key_ref, value_ref, grad_ref, out_ref, stat_ref, sum_ref,
    grad_query_ref, grad_pair_ref,
    key_rows, value_rows, query_rows, grad_rows, query_more, grad_more, query_sum,
):
    size = HEAD_DIM
    tokens = query_ref.shape[2]
    keys_held = key_ref.shape[2]
    queries = query_ref[0] * jnp.array(size ** (-0.5), LOW)
    grads = grad_ref[0]
    ones = jnp.where(lax.broadcasted_iota(jnp.int32, (keys_held, size), 1) < 3, 1.0, 0.0).astype(LOW)
    key_rows[:, :size] = key_ref[0].T
    key_rows[:, size:] = ones
    value_rows[:, :size] = value_ref[0].T
    value_rows[:, size:] = ones
    query_rows[...] = queries.T
    grad_rows[...] = grads.T
    inner = jnp.sum(grads.astype(WIDE) * out_ref[0].astype(WIDE), 0, keepdims=True)
    query_more[...] = with_parts(queries, -stat_ref[0])
    grad_more[...] = with_parts(grads, -inner)
    query_sum[...] = jnp.zeros_like(query_sum) if first else sum_ref[0]

    def step(index, carry):
        place = pl.ds(pl.multiple_of(index * key_block, key_block), key_block)
        keys, values, columns = key_rows[place, :], value_rows[place, :], key_ref[0, :, place]
        key_sum = jnp.zeros((key_block, size), WIDE)
        value_sum = jnp.zeros((key_block, size), WIDE)
        for part in range(tokens // query_block):
            span = slice(part * query_block, (part + 1) * query_block)
            probs = jnp.exp(jnp.dot(keys, query_more[:, span], preferred_element_type=WIDE))
            centered = jnp.dot(values, grad_more[:, span], preferred_element_type=WIDE)
            grad_scores = (probs * centered).astype(LOW)
            value_sum += jnp.dot(probs.astype(LOW), grad_rows[span, :], preferred_element_type=WIDE)
            key_sum += jnp.dot(grad_scores, query_rows[span, :], preferred_element_type=WIDE)
            query_sum[:, span] += jnp.dot(columns, grad_scores, preferred_element_type=WIDE)
        grad_pair_ref[0, :size, place] = key_sum.T.astype(LOW)
        grad_pair_ref[0, size:, place] = value_sum.T.astype(LOW)
        return carry

    lax.fori_loop(0, keys_held // key_block, step, 0)
    if first:
        grad_query_ref[0] = query_sum[...]
    else:
        grad_query_ref[0] = (query_sum[...] * size ** (-0.5)).astype(LOW)


def attend_back(head, near_rows, pair_rows, key_place, grads, outs, stats, query_sum, before=(), through=()):
    tokens = near_rows.shape[2]
    size = HEAD_DIM
    key_block, query_block = math.gcd(tokens, 1024), math.gcd(tokens, 512)
    first = query_sum is None
    if first:
        query_sum = jnp.zeros((1, 8, 128), WIDE)

    def rows(count, place=0):
        return pl.BlockSpec((1, count, tokens), lambda i: (head, place, 0))

    def result(count):
        return pl.BlockSpec((1, count, tokens), lambda i: (0, 0, 0))

    return ordered_call(
        functools.partial(attend_back_kernel, key_block, query_block, first),
        (near_rows, pair_rows, pair_rows, grads, outs, stats, query_sum),
        grid=(1,),
        in_specs=[
            rows(size),
            rows(size, key_place),
            rows(size, key_place + 1),
            rows(size),
            rows(size),
            rows(1),
            pl.BlockSpec(query_sum.shape, lambda i: (0, 0, 0)),
        ],
        out_specs=[result(size), result(2 * size)],
        out_shape=[
            jax.ShapeDtypeStruct((1, size, tokens), WIDE if first else LOW),
            jax.ShapeDtypeStruct((1, 2 * size, tokens), LOW),
        ],
        scratch_shapes=[
            pltpu.VMEM((tokens, 2 * size), LOW),
            pltpu.VMEM((tokens, 2 * size), LOW),
            pltpu.VMEM((tokens, size), LOW),
            pltpu.VMEM((tokens, size), LOW),
            pltpu.VMEM((2 * size, tokens), LOW),
            pltpu.VMEM((2 * size, tokens), LOW),
            pltpu.VMEM((size, tokens), WIDE),
        ],
        compiler_params=pltpu.CompilerParams(vmem_limit_bytes=48 * 2**20),
        cost_estimate=pl.CostEstimate(
            flops=tokens * tokens * size * 10 * 4,
            bytes_accessed=size * tokens * 2 * 9,
            transcendentals=tokens * tokens,
        ),
        before=before,
        through=through,
    )


def weight_kernel(
    normed_ref, hidden_ref, far_hidden_ref, feed_ref, active_ref, far_active_ref, branch_ref, heads_ref,
    near_ref, far_ref,
    normed_columns, feed_columns, branch_columns,
):
    @pl.when(pl.program_id(0) == 0)
    def _():
        normed_columns[...] = normed_ref[...].T
        feed_columns[...] = feed_ref[...].T
        branch_columns[...] = branch_ref[...].T

    units, features = hidden_ref.shape[1], heads_ref.shape[0]
    merger = dot_wide(branch_columns[...], heads_ref[...], 1, 1).astype(LOW)
    for made_ref, hidden, active in (
        (near_ref, hidden_ref, active_ref),
        (far_ref, far_hidden_ref, far_active_ref),
    ):
        for start, left, right in ((0, normed_columns, hidden), (units, feed_columns, active)):
            made_ref[:, start : start + units] = jnp.dot(
                left[...], right[...], preferred_element_type=WIDE
            ).astype(LOW)
        made_ref[:, 2 * units :] = jnp.zeros((made_ref.shape[0], made_ref.shape[1] - 2 * units), LOW)
        made_ref[:, 2 * units : 2 * units + features] = merger


def padded_columns(count):
    return -(-count // 128) * 128


def weight_terms(normed, grad_hidden, grad_feed, activated, grad_branch, attended, steps):
    tokens, width = normed.shape
    units, features = grad_hidden[0].shape[1] // steps, attended.shape[0] // steps
    columns = padded_columns(2 * units + features)

    def whole(array):
        return pl.BlockSpec(array.shape, lambda i: (0, 0))

    taken = pl.BlockSpec((tokens, units), lambda i: (0, i))
    made = pl.BlockSpec((width, columns), lambda i: (0, i))
    return pl.pallas_call(
        weight_kernel,
        grid=(steps,),
        in_specs=[whole(normed), taken, taken, whole(grad_feed), taken, taken]
        + [whole(grad_branch), pl.BlockSpec((features, tokens), lambda i: (i, 0))],
        out_specs=[made] * 2,
        out_shape=[jax.ShapeDtypeStruct((width, steps * columns), LOW)] * 2,
        scratch_shapes=[pltpu.VMEM((width, tokens), LOW)] * 3,
        compiler_params=pltpu.CompilerParams(vmem_limit_bytes=48 * 2**20),
        cost_estimate=pl.CostEstimate(
            flops=2 * tokens * width * steps * (4 * units + features),
            bytes_accessed=2**25,
            transcendentals=0,
        ),
    )(normed, *grad_hidden, grad_feed, *activated, grad_branch, attended)


def core_half(grad):
    ctx_size, shard_size = lax.axis_size("ctx"), lax.axis_size("shard")
    rows = grad.shape[0] // (shard_size * ctx_size)
    low = grad.astype(LOW).reshape(shard_size, ctx_size, rows, grad.shape[1])
    core = lax.axis_index("ctx")
    mine = lax.dynamic_index_in_dim(low, core, 1, keepdims=False)
    theirs = lax.dynamic_index_in_dim(low, 1 - core, 1, keepdims=False)
    return (
        mine.reshape(shard_size * rows, grad.shape[1]),
        theirs.reshape(shard_size * rows, grad.shape[1]),
    )


def sum_low(left, right):
    return (left.astype(WIDE) + right.astype(WIDE)).astype(LOW)


def shards(
    latent,
    condition,
    modulator,
    modulator_bias,
    projector,
    projector_bias,
    merger,
    merger_bias,
    expander,
    expander_bias,
    reducer,
    reducer_bias,
    cotangent,
):
    tp_size, ctx_size, shard_size = (lax.axis_size(axis) for axis in ("tp", "ctx", "shard"))
    core = lax.axis_index("ctx")
    own_latent, own_cotangent = latent[0], cotangent[0]
    block, model_width = own_latent.shape
    local_width = projector.shape[2]
    heads = local_width // HEAD_DIM
    head_columns = 3 * HEAD_DIM
    local_hidden = expander.shape[1]
    half_hidden = local_hidden // ctx_size
    kept_rows = projector.shape[0]
    place = lax.axis_index("shard") * kept_rows

    conditions = jnp.concatenate(mirror_gather(condition.astype(WIDE)), 0)
    def half_units(weight, axis):
        return lax.dynamic_slice_in_dim(weight, core * half_hidden, half_hidden, axis)

    share = tp_size * half_hidden
    latent_blocks = gather_list(own_latent, "tp")
    own_reducer = lax.all_gather(
        jnp.concatenate(gather_list(half_units(reducer, 0).T, "tp"), 1), "shard", axis=0, tiled=True
    )

    scaled_all = silu_gate(conditions).astype(LOW)
    terms = jnp.dot(
        lax.dynamic_slice_in_dim(scaled_all, place, kept_rows, 1),
        modulator,
        preferred_element_type=WIDE,
    )
    terms = mirror_exchange([terms[r : r + 1] for r in range(shard_size)])
    modulation = tree_sum(terms) + modulator_bias.astype(WIDE)

    own_projector = (
        projector.reshape(kept_rows, 3, heads, HEAD_DIM)
        .transpose(0, 2, 1, 3)
        .reshape(kept_rows, 3 * local_width)
    )
    head_projector = jnp.concatenate(in_shard_order(mirror_gather(own_projector)), 0)
    zero_bias = jnp.zeros((1, local_width), projector_bias.dtype)
    qkv_bias = (
        jnp.concatenate([projector_bias[:1], zero_bias, projector_bias[1:]], 0)
        .reshape(3, heads, HEAD_DIM)
        .transpose(1, 0, 2)
        .reshape(3 * local_width, 1)
        .astype(WIDE)
    )
    settings = [
        modulation[:, index * model_width : (index + 1) * model_width] for index in range(6)
    ]
    shift_one, scale_one, gate_one, shift_two, scale_two, gate_two = settings

    latent_blocks = [latent_blocks[0], *tie(latent_blocks[1:], head_projector, modulation)]
    normed_rows = jnp.concatenate(
        [modulate(rows.astype(WIDE), scale_one, shift_one).astype(LOW) for rows in latent_blocks], 0
    )
    tokens = normed_rows.shape[0]
    projected = (dot_wide(head_projector, normed_rows, 0, 1) + qkv_bias).astype(LOW)
    near_rows = projected.reshape(heads, head_columns, tokens)
    far_rows = swap_ctx(near_rows[:, HEAD_DIM:, :])

    bias_rows = jnp.zeros((16, half_hidden + local_width), expander_bias.dtype)
    for index, part in enumerate((core, 1 - core)):
        half_bias = lax.dynamic_slice_in_dim(expander_bias, part * half_hidden, half_hidden, 0)
        bias_rows = bias_rows.at[index, :half_hidden].set(half_bias)
    pieces = jnp.concatenate([half_units(expander, 1), merger.T], 1)
    pieces = jnp.concatenate([pieces, bias_rows], 0)
    pieces = gather_list(tie([pieces], *latent_blocks[1:])[0], "tp")
    pieces = tie(pieces, near_rows)
    own_expander = lax.all_gather(
        jnp.concatenate([piece[:kept_rows, :half_hidden] for piece in pieces], 1),
        "shard",
        axis=0,
        tiled=True,
    )
    full_merger = lax.all_gather(
        jnp.concatenate([piece[:kept_rows, half_hidden:] for piece in pieces], 1),
        "shard",
        axis=0,
        tiled=True,
    )
    part_biases = [
        jnp.concatenate(
            [piece[kept_rows + index : kept_rows + index + 1, :half_hidden] for piece in pieces], 1
        )
        for index in range(2)
    ]
    outs, stats, sent = [None] * tp_size, [None] * tp_size, [None] * tp_size
    order = sorted(range(tp_size), key=lambda r: -min(r, tp_size - r))
    previous = ()
    for r in order:
        (outs[r], stats[r]), _ = attend(near_rows, far_rows, r, block, previous)
        sent[r] = outs[r].reshape(local_width, block)
        previous = (outs[r],)
    attended = jnp.concatenate(scatter_list(sent, "tp"), 0)
    all_outs, all_stats = jnp.concatenate(outs, 2), jnp.concatenate(stats, 2)

    own_expander, full_merger = tie([own_expander, full_merger], outs[order[-1]])
    expanders = [own_expander, swap_ctx(own_expander)]
    reducers = [own_reducer, swap_ctx(own_reducer)]
    core_width = model_width // ctx_size
    tail_projector = lax.dynamic_slice_in_dim(head_projector, core * core_width, core_width, 0).T
    projectors = lax.all_gather(
        tie([tail_projector], outs[order[-1]])[0], "tp", axis=0, tiled=True
    )
    latent_wide = own_latent.astype(WIDE)
    branch = dot_wide(attended, full_merger, 0, 1) + merger_bias.astype(WIDE)
    middle = latent_wide + gate_one * branch
    normed_two_wide, norm_back_two = jax.vjp(modulate, middle, scale_two, shift_two)
    normed_two = normed_two_wide.astype(LOW)
    grad_output = own_cotangent.astype(WIDE)
    grad_feed = (gate_two * grad_output).astype(LOW)
    feed, grad_normed_two = reducer_bias.astype(WIDE), 0.0
    activated, grad_hidden = [], []
    for full_expander, full_reducer, part_bias in zip(expanders, reducers, part_biases):
        hidden = dot_wide(normed_two, full_expander, 1, 0) + part_bias.astype(WIDE)
        active, gelu_back = jax.vjp(gelu_tanh, hidden)
        activated.append(active.astype(LOW))
        feed = feed + dot_wide(activated[-1], full_reducer, 1, 1)
        grad_hidden.append(gelu_back(dot_wide(grad_feed, full_reducer, 1, 0))[0].astype(LOW))
        grad_normed_two = grad_normed_two + dot_wide(grad_hidden[-1], full_expander, 1, 1)
    block_output = (middle + gate_two * feed).astype(LOW)
    grad_gate_two = jnp.sum(grad_output * feed, 0, keepdims=True)
    grad_middle_norm, grad_scale_two, grad_shift_two = norm_back_two(grad_normed_two)
    grad_middle = grad_output + grad_middle_norm
    grad_gate_one = jnp.sum(grad_middle * branch, 0, keepdims=True)
    grad_branch = (gate_one * grad_middle).astype(LOW)
    grad_attended = dot_wide(full_merger, grad_branch, 0, 1).astype(LOW)
    grad_blocks = scatter_list(
        [grad_attended[r * local_width : (r + 1) * local_width] for r in range(tp_size)], "tp"
    )

    weight_near, weight_far = weight_terms(
        normed_two, grad_hidden, grad_feed, activated, grad_branch, attended, tp_size
    )
    all_grads = jnp.concatenate(grad_blocks, 1).reshape(heads, HEAD_DIM, tokens)

    def in_order(left, right, axis):
        return jnp.where(
            core == 0, jnp.concatenate([left, right], axis), jnp.concatenate([right, left], axis)
        )

    tp_turn = lax.rem(tp_size - lax.axis_index("tp"), tp_size)
    hidden_sums = in_order(
        *(jnp.sum(part, 0, dtype=WIDE).reshape(tp_size, half_hidden) for part in grad_hidden), 1
    )
    early_sums = jnp.concatenate(
        [
            grad_gate_one,
            grad_shift_two,
            grad_scale_two,
            grad_gate_two,
            jnp.sum(grad_feed, 0, keepdims=True, dtype=WIDE),
            jnp.sum(grad_branch, 0, keepdims=True, dtype=WIDE),
            rotated(hidden_sums, tp_turn),
        ],
        0,
    )

    def projector_half(rows):
        own, other = core_half(dot_wide(normed_rows, jnp.concatenate(rows, 0), 0, 1))
        return sum_low(own, swap_ctx(other))

    head_rows, arrived_rows = [], []
    for head in range(heads):
        before = ()
        if head == 1:
            before = (head_rows[0],)
        elif head == 2:
            before = (head_rows[1], *arrived_rows[0])
        (partial, far), _ = attend_back(
            head, near_rows, far_rows, 0, all_grads, all_outs, all_stats, None, before
        )
        before = ()
        if head == 0:
            (weight_came,) = tie([swap_ctx(weight_far)], partial)
            weight_half = sum_low(weight_near, weight_came)
            weight_sum = lax.psum_scatter(weight_half, "shard", scatter_dimension=0, tiled=True)
            before = (weight_half,)
        elif head == 1:
            projectors = tie([projectors], partial)[0]
            other_projectors = swap_ctx(projectors)
        elif head == 2:
            early_projector = projector_half(head_rows)
            before = (other_projectors, *arrived_rows[1], early_projector)
        far_came = swap_ctx(far[0])
        (grad_query, near), _ = attend_back(
            head, near_rows, near_rows, 1, all_grads, all_outs, all_stats, partial, before
        )
        rows = jnp.concatenate([grad_query[0], sum_low(near[0], far_came)], 0)
        head_rows.append(rows)
        arrived_rows.append(
            scatter_list([rows[:, r * block : (r + 1) * block] for r in range(tp_size)], "tp")
        )
    rows = jnp.zeros((tp_size * heads * head_columns, block), LOW)
    for head, arrived in enumerate(arrived_rows):
        for r, part in enumerate(arrived):
            turn = lax.rem(lax.axis_index("tp") + r, tp_size)
            rows = lax.dynamic_update_slice_in_dim(
                rows, part, (turn * heads + head) * head_columns, 0
            )
    grad_normed = in_order(
        *(dot_wide(rows, part, 0, 0) for part in (projectors, other_projectors)), 1
    )
    _, norm_back = jax.vjp(modulate, latent_wide, scale_one, shift_one)
    grad_latent_norm, grad_scale_one, grad_shift_one = norm_back(grad_normed)
    grad_latent = grad_middle + grad_latent_norm

    def from_peers(columns):
        width = columns.shape[1] // tp_size
        parts = scatter_list([columns[:, r * width : (r + 1) * width] for r in range(tp_size)], "tp")
        return sum(part.astype(WIDE) for part in parts)

    row_count = kept_rows // ctx_size
    summed = from_peers(weight_sum)
    two = summed[:, : 2 * half_hidden]
    own_two = lax.dynamic_slice_in_dim(two, core * row_count, row_count, 0)
    other_two = swap_ctx(lax.dynamic_slice_in_dim(two, (1 - core) * row_count, row_count, 0))
    grad_expander = in_order(own_two[:, :half_hidden], other_two[:, :half_hidden], 1)
    grad_reducer = in_order(own_two[:, half_hidden:], other_two[:, half_hidden:], 1).T
    grad_merger = lax.dynamic_slice_in_dim(summed[:, 2 * half_hidden : 2 * half_hidden + local_width], core * row_count, row_count, 0).T

    column_sums = jnp.sum(jnp.concatenate(head_rows, 0), 1, dtype=WIDE).reshape(heads, 3, HEAD_DIM)
    bias_sums = jnp.stack([column_sums[:, 0].reshape(-1), column_sums[:, 2].reshape(-1)])
    bias_sums = lax.dynamic_update_slice_in_dim(
        jnp.zeros((2, model_width), WIDE), bias_sums, lax.axis_index("tp") * local_width, 1
    )
    sums = jnp.concatenate([grad_shift_one, grad_scale_one, early_sums, bias_sums], 0)
    all_sums = mirror_gather(sum_over(sums, ("ctx", "tp")))
    total = tree_sum(all_sums)

    projector_sums = [
        lax.psum_scatter(half, "shard", scatter_dimension=0, tiled=True)
        for half in (early_projector, projector_half(head_rows[-1:]))
    ]
    grad_projector = jnp.concatenate(tie(projector_sums, *all_sums[1:]), 1)
    grad_projector = (
        grad_projector.astype(WIDE)
        .reshape(-1, heads, 3, HEAD_DIM)
        .transpose(0, 2, 1, 3)
        .reshape(-1, 3, local_width)
    )

    hidden_bias = lax.dynamic_index_in_dim(total[8:-2], lax.axis_index("tp"), 0, keepdims=False)
    projector_bias_sums = lax.dynamic_slice_in_dim(
        total[-2:], lax.axis_index("tp") * local_width, local_width, 1
    )
    total_settings = total[:6].reshape(-1)
    all_settings = jnp.concatenate([part[:6] for part in all_sums], 0).reshape(shard_size, -1)
    gate_terms = lax.dot_general(
        all_settings, modulator.astype(WIDE), (((1,), (1,)), ((), ())), precision=PRECISE
    )
    gate_terms = in_shard_order(mirror_exchange([gate_terms[r : r + 1] for r in range(shard_size)]))
    _, silu_back = jax.vjp(silu_gate, condition.astype(WIDE))
    grad_condition = silu_back(jnp.concatenate(gate_terms, 1))[0]
    column_count = all_settings.shape[1] // tp_size
    tp_settings = lax.dynamic_slice_in_dim(
        all_settings, lax.axis_index("tp") * column_count, column_count, 1
    )
    tp_scaled = lax.dynamic_slice_in_dim(
        scaled_all.astype(WIDE), place + core * row_count, row_count, 1
    )
    grad_modulator = lax.dot_general(
        tp_scaled, tp_settings, (((0,), (0,)), ((), ())), precision=PRECISE
    )
    grad_modulator_bias = lax.dynamic_slice_in_dim(
        total_settings, lax.axis_index("tp") * column_count, column_count, 0
    )
    return (
        block_output[None],
        grad_latent[None],
        grad_condition,
        grad_modulator,
        grad_modulator_bias,
        grad_projector,
        projector_bias_sums,
        grad_merger,
        total[7],
        grad_expander,
        hidden_bias,
        grad_reducer,
        total[6],
    )


def solution(mesh):
    in_specs = (
        P("shard", ("ctx", "tp"), None),
        P("shard", None),
        P("shard", None),
        P(),
        P("shard", None, "tp"),
        P(None, "tp"),
        P("tp", "shard"),
        P(),
        P("shard", "tp"),
        P("tp"),
        P("tp", "shard"),
        P(),
        P("shard", ("ctx", "tp"), None),
    )
    out_specs = (
        P("shard", ("ctx", "tp"), None),
        P("shard", ("ctx", "tp"), None),
        P("shard", None),
        P(("shard", "ctx"), "tp"),
        P("tp"),
        P(("shard", "ctx"), None, "tp"),
        P(None, "tp"),
        P("tp", ("shard", "ctx")),
        P(),
        P(("shard", "ctx"), "tp"),
        P("tp"),
        P("tp", ("shard", "ctx")),
        P(),
    )
    return jax.shard_map(shards, mesh=mesh, in_specs=in_specs, out_specs=out_specs, check_vma=False)
```
